256 devices in a mesh: gx: 32 (over y_hi, z, core), gy: 8 (over x, y_lo).
Axes of the slice: x: 4, y: 4 (y_hi: 2, y_lo: 2; y = y_hi * 2 + y_lo), z: 8, core: 2. Of those that a mesh axis runs over, the one named last changes fastest.
Arguments:
- pressure_head: float32 [32, 128, 1024], P('gx', None, 'gy'), may hold values from -0.8 to -0.1
- material_zone: int32 [32, 128, 1024], P('gx', None, 'gy'), may hold values from 0 to 3
- emitters: int32 [32, 1024], P('gx', 'gy'), may hold values 0 or 1
- oxygen: float32 [32, 128, 1024], P('gx', None, 'gy'), may hold values from 0.05 to 1
- sulfide_rate: float32 [32, 128, 1024], P('gx', None, 'gy'), may hold values from 0.05 to 0.5
- air_flux: float32 [32, 1024], P('gx', 'gy'), may hold values from 0.02 to 0.3
Outputs:
- head_out: float32 [32, 128, 1024], P('gx', None, 'gy')
- oxygen_out: float32 [32, 128, 1024], P('gx', 'gy')
The draws below stay inside these ranges and needn't reach their ends.
Inputs may be any that keep to these rules, and one draw needn't show every extreme that they name: `material_zone`: material zones index the four parameter sets.
All inputs are finite; a program needn't handle non-finite values. No bound on the sum of `emitters` on one device may be relied on, other than what follows from the above.
Results may differ from the reference program's by a relative error of at most 0.0003.
Values sent between devices are 32-bit elements; how exact they have to be, the bound alone decides.
A program may use at most 64 MiB of HBM per device.

```python
import math
import jax
import jax.numpy as jnp
from jax import lax

NZ = 128
PICARD = 2
SWEEPS = 8
GAS_STEPS = 2
ZONES = 4
NX = 32
NY = 1024


def touch_ends(values, stream_key, least, high):
    shape = values.shape
    spot = [jax.random.randint(jax.random.fold_in(stream_key, axis), (), 0, shape[axis]) for axis in range(len(shape))]
    values = values.at[tuple(spot)].set(least)
    longest = shape.index(max(shape))
    spot[longest] = (spot[longest] + 1) % shape[longest]
    return values.at[tuple(spot)].set(high)


def block_levels(key, dims, split, smallest, largest):
    loudness = 1.0
    for position, parts in split:
        draws = jax.random.uniform(jax.random.fold_in(jax.random.fold_in(key, 6), position), (parts,), jnp.float32, smallest / len(split), largest / len(split))
        loudness = loudness * jnp.repeat(jnp.exp(draws), dims[position] // parts).reshape((-1,) + (1,) * (len(dims) - 1 - position))
    return loudness


def setup_inputs(seed: int = 0) -> dict:
    keys = jax.random.split(jax.random.key(seed), 7)
    return {
        "pressure_head": jnp.clip(-0.8 + 0.7 * jax.random.uniform(keys[0], (NX, NZ, NY), jnp.float32) ** block_levels(keys[0], (NX, NZ, NY), ((0, 32), (2, 8)), -0.2, 0.2), -0.8, -0.1),
        "material_zone": touch_ends(jax.random.randint(keys[1], (NX, NZ, NY), 0, ZONES), jax.random.fold_in(keys[1], 1), 0, ZONES - 1).astype(jnp.int32),
        "emitters": touch_ends((jax.random.randint(keys[2], (NX, NY), 0, 3) < 1).astype(jnp.int32), jax.random.fold_in(keys[2], 1), 0, 1),
        "oxygen": jnp.clip(0.05 + 0.95 * jax.random.uniform(keys[3], (NX, NZ, NY), jnp.float32) ** block_levels(keys[3], (NX, NZ, NY), ((0, 32), (2, 8)), -0.2, 0.2), 0.05, 1.0),
        "sulfide_rate": jnp.clip(jnp.exp(math.log(0.5) - 2.3025851 * jax.random.uniform(keys[4], (NX, NZ, NY), jnp.float32) ** block_levels(keys[4], (NX, NZ, NY), ((0, 32), (2, 8)), -0.2, 0.2)), 0.05, 0.5),
        "air_flux": jnp.clip(jnp.exp(math.log(0.3) - 2.7080503 * jax.random.uniform(keys[5], (NX, NY), jnp.float32) ** block_levels(keys[5], (NX, NY), ((0, 32), (1, 8)), -0.2, 0.2)), 0.02, 0.3),
    }


TABLE = ((4.0, 2.5, 1.2, 0.8), (2.4, 1.9, 1.6, 1.4), (0.05, 0.08, 0.1, 0.12), (0.38, 0.42, 0.45, 0.4), (5.0, 2.0, 0.6, 0.2))
flow_step = 2.0
storage_term = 0.01
cond_floor = 0.001
irrigation = 0.3
gas_step = 0.25

def zone_params(material_zone):
    result = []
    for entries in TABLE:
        selected = jnp.zeros(material_zone.shape, jnp.float32)
        for number in range(4):
            selected = selected + jnp.where(material_zone == number, jnp.float32(entries[number]), jnp.float32(0.0))
        result.append(selected)
    return result

def retention(head_field, params):
    entry_scale, pore_index, residual_water, saturated_water, saturated_cond = params
    suction = jnp.maximum(-head_field, 0.0)
    exponent = 1.0 - 1.0 / pore_index
    scaled = entry_scale * suction
    powered = scaled ** pore_index
    effective = (1.0 + powered) ** (-exponent)
    water_content = residual_water + (saturated_water - residual_water) * effective
    capacity = (saturated_water - residual_water) * entry_scale * pore_index * exponent * scaled ** (pore_index - 1.0) * (1.0 + powered) ** (-exponent - 1.0) + storage_term
    mualem_term = 1.0 - (1.0 - effective ** (1.0 / exponent)) ** exponent
    conductivity = saturated_cond * (jnp.sqrt(effective) * mualem_term * mualem_term + cond_floor)
    return (water_content, capacity, conductivity, effective)

def harmonic(first, second):
    return 2.0 * first * second / (first + second)

def shift_down(values, stride, filler):
    edge = jnp.full((values.shape[0], stride, values.shape[2]), filler, values.dtype)
    return jnp.concatenate([edge, values[:, :-stride]], axis=1)

def shift_up(values, stride, filler):
    edge = jnp.full((values.shape[0], stride, values.shape[2]), filler, values.dtype)
    return jnp.concatenate([values[:, stride:], edge], axis=1)

def neighbours(padded):
    return (padded[:-2, :, 1:-1], padded[2:, :, 1:-1], padded[1:-1, :, :-2], padded[1:-1, :, 2:])

def swap_depth(values):
    return jnp.swapaxes(values, 1, 2)

def column_solve(below_diag, main_diag, above_diag, source):
    solved = lax.linalg.tridiagonal_solve(swap_depth(below_diag), swap_depth(main_diag), swap_depth(above_diag), swap_depth(source)[..., None])
    return swap_depth(solved[..., 0])

def gas_update(conc_full, diff_full, oxygen_now, diffusivity, reaction, storage, upward, top_rows, bottom):
    sides = [(slice(None, -2), slice(1, -1), slice(1, -1)), (slice(2, None), slice(1, -1), slice(1, -1)), (slice(1, -1), slice(None, -2), slice(1, -1)), (slice(1, -1), slice(2, None), slice(1, -1)), (slice(1, -1), slice(1, -1), slice(None, -2)), (slice(1, -1), slice(1, -1), slice(2, None))]
    diffusive = jnp.zeros_like(oxygen_now)
    for window in sides:
        diffusive = diffusive + jnp.sqrt(diffusivity * diff_full[window]) * (conc_full[window] - oxygen_now)
    below_cell = conc_full[1:-1, 2:, 1:-1] + bottom
    change = diffusive + 2.0 * diffusivity * (1.0 - oxygen_now) * top_rows + upward * (below_cell - oxygen_now) - reaction * oxygen_now
    return oxygen_now + storage * change

def reference(pressure_head, material_zone, emitters, oxygen, sulfide_rate, air_flux):
    params = zone_params(material_zone)
    theta_old = retention(pressure_head, params)[0]
    depth = pressure_head.shape[1]
    layer_index = lax.broadcasted_iota(jnp.int32, pressure_head.shape, 1)
    top_rows = (layer_index == 0).astype(pressure_head.dtype)
    bottom = (layer_index == depth - 1).astype(pressure_head.dtype)
    irrigated = top_rows * irrigation * emitters[:, None, :].astype(pressure_head.dtype)
    lateral_pad = ((1, 1), (0, 0), (1, 1))
    current = pressure_head
    for picard_pass in range(PICARD):
        theta_now, capacity, conductivity, effective = retention(current, params)
        lateral = [harmonic(conductivity, other) for other in neighbours(jnp.pad(conductivity, lateral_pad))]
        upper_face = harmonic(conductivity, shift_down(conductivity, 1, 0.0))
        lower_face = harmonic(conductivity, shift_up(conductivity, 1, 0.0))
        diagonal = capacity / flow_step + lateral[0] + lateral[1] + lateral[2] + lateral[3] + upper_face + lower_face
        base_source = capacity / flow_step * current - (theta_now - theta_old) / flow_step + upper_face - lower_face - bottom * conductivity + irrigated
        iterate = current
        for sweep_pass in range(SWEEPS):
            beside_all = neighbours(jnp.pad(iterate, lateral_pad))
            source = base_source + lateral[0] * beside_all[0] + lateral[1] * beside_all[1] + lateral[2] * beside_all[2] + lateral[3] * beside_all[3]
            iterate = column_solve(-upper_face, diagonal, -lower_face, source)
        current = iterate
    theta_end, capacity, conductivity, effective = retention(current, params)
    gas_filled = (params[3] - params[2]) * (1.0 - effective)
    diffusivity = gas_filled ** (10.0 / 3.0) / (params[3] * params[3])
    reaction = sulfide_rate * theta_end / params[3]
    storage = gas_step / params[3]
    upward = jnp.broadcast_to(air_flux[:, None, :], current.shape)
    diff_full = jnp.pad(diffusivity, 1)
    oxygen_now = oxygen
    for gas_pass in range(GAS_STEPS):
        oxygen_now = gas_update(jnp.pad(oxygen_now, 1), diff_full, oxygen_now, diffusivity, reaction, storage, upward, top_rows, bottom)
    return (current, oxygen_now)
```

```python
import jax
import jax.numpy as jnp
from jax import lax
from jax.experimental import pallas as pl
from jax.experimental.pallas import tpu as pltpu
from jax.sharding import PartitionSpec as P

SWEEPS = 8
TABLE = (
    (4.0, 2.5, 1.2, 0.8),
    (2.4, 1.9, 1.6, 1.4),
    (0.05, 0.08, 0.1, 0.12),
    (0.38, 0.42, 0.45, 0.4),
    (5.0, 2.0, 0.6, 0.2),
)
FLOW_STEP = 2.0
STORAGE_TERM = 0.01
COND_FLOOR = 0.001
IRRIGATION = 0.3
GAS_STEP = 0.25

NX, NYD, LANES, DEPTH, SEG, SUB = 32, 8, 128, 128, 16, 8
COLS = LANES // NX
STRIPS = NX * NYD
REGION = 5
MESH = pl.DeviceIdType.MESH

FWD = 0
BACK = 30
SCALE = 60
LAST = 67
NFAC = 74


def levels():
    result = []
    kept = list(range(SEG))
    place = 0
    scale = 0
    step = 1
    while len(kept) > 1:
        gone, stay = kept[0::2], kept[1::2]
        result.append((step, gone, stay, place, scale))
        place += len(gone)
        if step > 1:
            scale += len(gone)
        kept = stay
        step *= 2
    return result


LEVELS = levels()


def rows(j):
    return pl.ds(SUB * j, SUB)


def roll(x, shift, axis):
    return pltpu.roll(x, shift % x.shape[axis], axis)


def sel(masks, values):
    return jnp.where(
        masks[0],
        jnp.float32(values[0]),
        jnp.where(
            masks[1],
            jnp.float32(values[1]),
            jnp.where(masks[2], jnp.float32(values[2]), jnp.float32(values[3])),
        ),
    )


def zone_masks(zone):
    return (zone < 0.5, zone < 1.5, zone < 2.5)


def saturation(head, masks):
    a, n, r, s, k = TABLE
    au = sel(masks, a) * jnp.maximum(-head, 1e-37)
    power = jnp.exp2(sel(masks, [v - 1.0 for v in n]) * jnp.log2(au))
    one_p = 1.0 + power * au
    log_p = jnp.log2(one_p)
    m = sel(masks, [1.0 - 1.0 / v for v in n])
    return power, one_p, m * log_p


def harmonic(u, v):
    return 2.0 * u * v / (u + v)


def kernel(
    head_ref, zone_ref, em_ref, oxy_ref, sul_ref, flux_ref,
    head_out, oxy_out,
    tmp, tmp2, send_a, recv_a, send_b, recv_b, send_x, recv_x, reg_a, reg_b, reg_c, reg_d,
    cond, half_cap, se_old, base, lat, fac, x, gas_g, gas_f, gas_c, gas_r,
    send_h, recv_h, send_o, recv_o, brick,
    sems, halo_s, halo_r,
):
    g = lax.axis_index("gx")
    y = lax.axis_index("gy")

    def strip_of(gx):
        return gx + (gx // 16) * (47 - 2 * gx)

    s = strip_of(g)
    me = y * NX + s

    def device_of(strip):
        return (strip_of(strip % NX), strip // NX)

    lane = lax.broadcasted_iota(jnp.int32, (SUB, LANES), 1)
    sub = lax.broadcasted_iota(jnp.int32, (SUB, LANES), 0)
    plane = lane % NX
    col = lane // NX
    first_plane, last_plane = plane == 0, plane == NX - 1
    first_col, last_col = col == 0, col == COLS - 1
    top, bottom = sub == 0, sub == SUB - 1

    barrier = pltpu.get_barrier_semaphore()

    def greet_x(k, c):
        pl.semaphore_signal(barrier, inc=1, device_id=((g + k) % NX, y), device_id_type=MESH)
        return c

    def greet_y(k, c):
        pl.semaphore_signal(barrier, inc=1, device_id=(g, (y + k) % NYD), device_id_type=MESH)
        return c

    def valid(k):
        return jnp.logical_and(me + k >= 0, me + k < STRIPS)

    lax.fori_loop(1, NX, greet_x, 0)
    lax.fori_loop(1, NYD, greet_y, 0)
    for k in (-1, 1, -2, 2):
        @pl.when(jnp.logical_and(valid(k), jnp.logical_or(s + k < 0, s + k >= NX)))
        def _():
            pl.semaphore_signal(barrier, inc=1, device_id=device_of(me + k), device_id_type=MESH)

    def pack(first, second, out):
        for q in range(NX // 2):
            f = first[8 * q : 8 * q + 8]
            t = second[8 * q : 8 * q + 8]
            out[pl.ds(16 * q, 8), :] = jnp.where(sub < 4, f, roll(t, 4, 0))
            out[pl.ds(16 * q + 8, 8), :] = jnp.where(sub < 4, roll(f, 4, 0), t)

    def segmented(ref):
        return jnp.concatenate(
            [ref[0, pl.ds(j, SUB, stride=SEG), :].astype(jnp.float32) for j in range(SEG)], axis=0
        ).T

    pack(segmented(head_ref), segmented(zone_ref), send_a)
    send_x[0:1, :] = em_ref[...].astype(jnp.float32)
    send_x[1:2, :] = flux_ref[...]
    own = pl.ds(pl.multiple_of(8 * g, 8), 8)
    recv_a[own, :] = send_a[pl.ds(pl.multiple_of(8 * s, 8), 8), :]
    recv_x[g] = send_x[...]

    lower = (2 - jnp.minimum(s, 2)) * jnp.minimum(y, 1)
    upper = (2 - jnp.minimum(NX - 1 - s, 2)) * jnp.minimum(NYD - 1 - y, 1)
    pl.semaphore_wait(barrier, NX - 1 + NYD - 1 + lower + upper)

    def remote(src, dst, ssem, rsem, device):
        return pltpu.make_async_remote_copy(
            src_ref=src, dst_ref=dst, send_sem=ssem, recv_sem=rsem, device_id=device, device_id_type=MESH
        )

    def scatter8(src, dst, index):
        def body(k, c):
            tg = (g + k) % NX
            remote(
                src.at[pl.ds(pl.multiple_of(8 * strip_of(tg), 8), 8)],
                dst.at[pl.ds(pl.multiple_of(8 * g, 8), 8)],
                sems.at[0, index],
                sems.at[1, index],
                (tg, y),
            ).start()
            return c

        lax.fori_loop(1, NX, body, 0)

    def wait_all(part, sem):
        pltpu.make_async_copy(part, part, sem).wait()

    scatter8(send_a, recv_a, 0)

    def body_x(k, c):
        tg = (g + k) % NX
        remote(send_x, recv_x.at[g], sems.at[0, 1], sems.at[1, 1], (tg, y)).start()
        return c

    lax.fori_loop(1, NX, body_x, 0)

    pack(segmented(oxy_ref), segmented(sul_ref), send_b)
    recv_b[own, :] = send_b[pl.ds(pl.multiple_of(8 * s, 8), 8), :]

    most8 = pl.ds(0, 8 * (NX - 1))
    wait_all(recv_a.at[most8], sems.at[1, 0])

    def unpack(src, field):
        parts = [
            src[pl.ds(64 * q + 4 * field + c, 8, stride=8), :] for c in range(COLS) for q in range(NX // 8)
        ]
        return jnp.concatenate(parts, axis=0).T

    reg_a[2, 0:128, :] = unpack(recv_a, 0)
    reg_a[2, 128:256, :] = unpack(recv_a, 1)
    wait_all(recv_x.at[pl.ds(0, NX - 1)], sems.at[1, 1])
    tmp[0:32, :] = recv_x[:, 0, :]
    tmp[32:64, :] = recv_x[:, 1, :]
    tmp[64:128, :] = jnp.zeros((64, LANES), jnp.float32)
    tmp2[...] = tmp[...].T
    emitted = jnp.zeros((1, LANES), jnp.float32)
    fluxes = jnp.zeros((1, LANES), jnp.float32)
    lane1 = lax.broadcasted_iota(jnp.int32, (1, LANES), 1) // NX
    for c in range(COLS):
        row = tmp2[pl.ds(4 * s + c, 1), :]
        emitted = jnp.where(lane1 == c, roll(row, 32 * c, 1), emitted)
        fluxes = jnp.where(lane1 == c, roll(row, 32 * c - 32, 1), fluxes)
    reg_a[2, 256:264, :] = jnp.concatenate(
        [emitted, fluxes, jnp.zeros((6, LANES), jnp.float32)], axis=0
    )

    def halo(reg, index, middle, ks, start):
        for k in ks:
            there = middle - k

            @pl.when(valid(k))
            def _():
                copy = remote(
                    reg.at[middle],
                    reg.at[there],
                    halo_s.at[index, middle + k],
                    halo_r.at[index, there],
                    device_of(me + k),
                )
                if start:
                    copy.start()
                else:
                    copy.wait_send()

    def arrive(reg, index, middle, b):
        strip = me + b - middle
        inside = jnp.logical_and(strip >= 0, strip < STRIPS)

        @pl.when(inside)
        def _():
            pltpu.make_async_copy(reg.at[b], reg.at[b], halo_r.at[index, b]).wait()

        @pl.when(jnp.logical_not(inside))
        def _():
            reg[b] = reg[middle]

    halo(reg_a, 0, 2, (-1, 1, -2, 2), True)
    scatter8(send_b, recv_b, 2)

    def picard(reg, index, first):
        def retain(i, carry):
            step = (i + 1) // 2
            b = 2 + step * (1 - 2 * (i % 2))

            @pl.when(i > 0)
            def _():
                arrive(reg, index, 2, b)

            for j in range(SEG):
                h = reg[b, rows(j), :]
                masks = zone_masks(reg_a[b, pl.ds(128 + 8 * j, 8), :])
                power, one_p, mlog = saturation(h, masks)
                se = jnp.exp2(-mlog)
                a, n, r, sat, kk = TABLE
                filled = power * se
                cap = (
                    sel(masks, [(w - v) * p * q * (1.0 - 1.0 / q) / FLOW_STEP for p, q, v, w in zip(a, n, r, sat)])
                    * filled
                    / one_p
                    + STORAGE_TERM / FLOW_STEP
                )
                rest = 1.0 - filled
                cond[b, rows(j), :] = sel(masks, kk) * (jnp.exp2(-0.5 * mlog) * rest * rest + COND_FLOOR)
                half_cap[b, rows(j), :] = cap
                x[0, b, rows(j), :] = h
                if first:
                    se_old[b, rows(j), :] = se
                    base[b, rows(j), :] = cap * h
                else:
                    base[b, rows(j), :] = cap * h - sel(
                        masks, [(w - v) / FLOW_STEP for v, w in zip(r, sat)]
                    ) * (se - se_old[b, rows(j), :])
            return carry

        lax.fori_loop(0, REGION, retain, 0)

        def assemble(b, carry):
            after, before = jnp.minimum(b + 1, REGION - 1), jnp.maximum(b - 1, 0)
            strip = me + b - 2
            closed = jnp.logical_or(strip == -1, strip == STRIPS - 1)
            open_face = jnp.where(closed, 0.0, 1.0)
            right_mask = jnp.where(last_col, open_face, 1.0)
            ks = [cond[b, rows(j), :] for j in range(SEG)]
            ups = [harmonic(ks[j], ks[j - 1]) for j in range(1, SEG)]
            up0 = jnp.where(top, 0.0, harmonic(ks[0], roll(ks[SEG - 1], 1, 0)))
            ups = [up0] + ups
            los = ups[1:] + [roll(up0, -1, 0)]
            av, cv = [], []
            for j in range(SEG):
                k = ks[j]
                xp = jnp.where(last_plane, 0.0, harmonic(k, roll(k, -1, 1)))
                xm = roll(xp, 1, 1)
                yp = right_mask * harmonic(
                    k, roll(jnp.where(first_col, cond[after, rows(j), :], k), -NX, 1)
                )
                lat[b, 3, rows(j), :] = yp
                ym = roll(jnp.where(last_col, lat[before, 3, rows(j), :], yp), NX, 1)
                diag = half_cap[b, rows(j), :] + xp + xm + yp + ym + ups[j] + los[j]
                inv = 1.0 / diag
                rhs = base[b, rows(j), :] + ups[j] - los[j]
                if j == SEG - 1:
                    rhs = rhs - jnp.where(bottom, k, 0.0)
                if j == 0:
                    rhs = rhs + jnp.where(top, IRRIGATION * reg_a[b, pl.ds(256, 1), :], 0.0)
                base[b, rows(j), :] = rhs * inv
                lat[b, 0, rows(j), :] = xm * inv
                lat[b, 1, rows(j), :] = xp * inv
                lat[b, 2, rows(j), :] = ym * inv
                lat[b, 4, rows(j), :] = yp * inv
                av.append(ups[j] * inv)
                cv.append(los[j] * inv)

            def put(i, value):
                fac[b, rows(i), :] = value

            bv = [None] * SEG
            for step, gone, stay, place, scale in LEVELS:
                for i, e in enumerate(gone):
                    if step > 1:
                        rec = 1.0 / bv[e]
                        put(SCALE + scale + i, rec)
                        av[e] = av[e] * rec
                        cv[e] = cv[e] * rec
                        bv[e] = rec
                    put(BACK + place + i, av[e])
                    put(BACK + 15 + place + i, cv[e])
                new = {}
                for i, j in enumerate(stay):
                    up, dn = j - step, j + step
                    if dn < SEG:
                        a_dn, c_dn = av[dn], cv[dn]
                        r_dn = bv[dn] if step > 1 else None
                    else:
                        a_dn, c_dn = roll(av[dn - SEG], -1, 0), roll(cv[dn - SEG], -1, 0)
                        r_dn = roll(bv[dn - SEG], -1, 0) if step > 1 else None
                    diag = (bv[j] if step > 1 else 1.0) - av[j] * cv[up] - cv[j] * a_dn
                    alpha = av[j] * bv[up] if step > 1 else av[j]
                    gamma = cv[j] * r_dn if step > 1 else cv[j]
                    put(FWD + place + i, alpha)
                    put(FWD + 15 + place + i, gamma)
                    new[j] = (av[j] * av[up], diag, cv[j] * c_dn)
                for j in stay:
                    av[j], bv[j], cv[j] = new[j]
            a, d, c = av[SEG - 1], bv[SEG - 1], cv[SEG - 1]
            for i, step in enumerate((1, 2, 4)):
                alpha = a / roll(d, step, 0)
                gamma = c / roll(d, -step, 0)
                put(LAST + 2 * i, alpha)
                put(LAST + 2 * i + 1, gamma)
                d = d - alpha * roll(c, step, 0) - gamma * roll(a, -step, 0)
                a, c = alpha * roll(a, step, 0), gamma * roll(c, -step, 0)
            put(LAST + 6, 1.0 / d)
            return carry

        lax.fori_loop(0, REGION, assemble, 0)

        def relax(now, b):
            def get(i):
                return fac[b, rows(i), :]

            later = 1 - now
            f = []
            for j in range(SEG):
                v = x[now, b, rows(j), :]
                left = jnp.where(last_col, x[now, max(b - 1, 0), rows(j), :], v)
                right = jnp.where(first_col, x[now, min(b + 1, REGION - 1), rows(j), :], v)
                f.append(
                    base[b, rows(j), :]
                    + lat[b, 0, rows(j), :] * roll(v, 1, 1)
                    + lat[b, 1, rows(j), :] * roll(v, -1, 1)
                    + lat[b, 2, rows(j), :] * roll(left, NX, 1)
                    + lat[b, 4, rows(j), :] * roll(right, -NX, 1)
                )
            for step, gone, stay, place, scale in LEVELS:
                for i, j in enumerate(stay):
                    dn = f[j + step] if j + step < SEG else roll(f[j + step - SEG], -1, 0)
                    f[j] = f[j] + get(FWD + place + i) * f[j - step] + get(FWD + 15 + place + i) * dn
            v = f[SEG - 1]
            for i, step in enumerate((1, 2, 4)):
                v = v + get(LAST + 2 * i) * roll(v, step, 0) + get(LAST + 2 * i + 1) * roll(v, -step, 0)
            f[SEG - 1] = v * get(LAST + 6)
            wrapped = roll(f[SEG - 1], 1, 0)
            for step, gone, stay, place, scale in reversed(LEVELS):
                for i, e in enumerate(gone):
                    up = f[e - step] if e >= step else wrapped
                    src = f[e] * get(SCALE + scale + i) if step > 1 else f[e]
                    f[e] = src + get(BACK + place + i) * up + get(BACK + 15 + place + i) * f[e + step]
            for j in range(SEG):
                x[later, b, rows(j), :] = f[j]

        def wide(t, carry):
            for b in range(REGION):
                relax(t % 2, b)
            return carry

        def narrow(t, carry):
            for b in (1, 2, 3):
                relax(t % 2, b)
            return carry

        lax.fori_loop(0, 3, wide, 0)
        lax.fori_loop(3, 7, narrow, 0)
        relax(1, 2)

    picard(reg_a, 0, True)
    reg_c[2] = x[0, 2]
    halo(reg_c, 1, 2, (-1, 1, -2, 2), True)

    wait_all(recv_b.at[most8], sems.at[1, 2])
    reg_b[1, 0:128, :] = unpack(recv_b, 0)
    reg_b[1, 128:256, :] = unpack(recv_b, 1)
    halo(reg_b, 3, 1, (-1, 1), True)

    picard(reg_c, 1, False)
    reg_d[1] = x[0, 2]
    halo(reg_d, 2, 1, (-1, 1), True)

    def scatter4(src, dst, index):
        def body(k, c):
            tg = (g + k) % NX
            remote(src.at[tg], dst.at[s], sems.at[0, index], sems.at[1, index], (tg, y)).start()
            return c

        lax.fori_loop(1, NX, body, 0)

    def pack_planes(field, out, own_slot):
        tmp[...] = field.T
        for p in range(NX):
            out[p] = tmp[pl.ds(p, COLS, stride=NX), :]
        own_slot[s] = out[g]

    pack_planes(x[0, 2], send_h, recv_h)
    scatter4(send_h, recv_h, 3)

    def gas_prepare(i, carry):
        b = (i + 1) % 3

        @pl.when(i > 0)
        def _():
            arrive(reg_b, 3, 1, b)
            arrive(reg_d, 2, 1, b)

        strip = me + b - 1
        inside = jnp.where(jnp.logical_and(strip >= 0, strip < STRIPS), 1.0, 0.0)
        a, n, r, sat, kk = TABLE
        for j in range(SEG):
            masks = zone_masks(reg_a[b + 1, pl.ds(128 + 8 * j, 8), :])
            power, one_p, mlog = saturation(reg_d[b, rows(j), :], masks)
            se = jnp.exp2(-mlog)
            span = sel(masks, [w - v for v, w in zip(r, sat)])
            inv_s = sel(masks, [1.0 / w for w in sat])
            gas = jnp.maximum(span * (1.0 - se), 1e-37)
            root = jnp.exp2((5.0 / 3.0) * jnp.log2(gas)) * inv_s * inside
            conc = reg_b[b, rows(j), :]
            gas_g[b, rows(j), :] = root
            gas_f[0, b, rows(j), :] = root * conc
            gas_c[0, b, rows(j), :] = conc
            gas_r[b, rows(j), :] = reg_b[b, pl.ds(128 + 8 * j, 8), :] * (sel(masks, r) + span * se) * inv_s
            gas_r[b, pl.ds(128 + 8 * j, 8), :] = GAS_STEP * inv_s
        return carry

    lax.fori_loop(0, 3, gas_prepare, 0)

    def gas_advance(step, b):
        before, after = jnp.maximum(b - 1, 0), jnp.minimum(b + 1, 2)

        def total(get, j):
            v = get(b, j)
            left = jnp.where(last_col, get(before, j), v)
            right = jnp.where(first_col, get(after, j), v)
            above = get(b, j - 1) if j > 0 else jnp.where(top, 0.0, roll(get(b, SEG - 1), 1, 0))
            below = get(b, j + 1) if j < SEG - 1 else jnp.where(bottom, 0.0, roll(get(b, 0), -1, 0))
            return (
                jnp.where(first_plane, 0.0, roll(v, 1, 1))
                + jnp.where(last_plane, 0.0, roll(v, -1, 1))
                + roll(left, NX, 1)
                + roll(right, -NX, 1)
                + above
                + below
            )

        flux = reg_a[b + 1, pl.ds(257, 1), :]
        for j in range(SEG):
            conc = gas_c[step, b, rows(j), :]
            root = gas_g[b, rows(j), :]
            sum_f = total(lambda bb, jj: gas_f[step, bb, rows(jj), :], j)
            sum_g = total(lambda bb, jj: gas_g[bb, rows(jj), :], j)
            if j < SEG - 1:
                under = gas_c[step, b, rows(j + 1), :]
            else:
                under = jnp.where(bottom, 1.0, roll(gas_c[step, b, rows(0), :], -1, 0))
            change = root * (sum_f - conc * sum_g) + flux * (under - conc) - gas_r[b, rows(j), :] * conc
            if j == 0:
                change = change + jnp.where(top, 2.0 * root * root * (1.0 - conc), 0.0)
            new = conc + gas_r[b, pl.ds(128 + 8 * j, 8), :] * change
            gas_c[step + 1, b, rows(j), :] = new
            if step == 0:
                gas_f[1, b, rows(j), :] = root * new

    def gas_first(b, carry):
        gas_advance(0, b)
        return carry

    lax.fori_loop(0, 3, gas_first, 0)
    gas_advance(1, 1)

    pack_planes(gas_c[2, 1], send_o, recv_o)
    scatter4(send_o, recv_o, 4)

    def planes(src):
        return jnp.concatenate([src[i] for i in range(NX)], axis=0).T

    most4 = pl.ds(0, NX - 1)
    wait_all(recv_h.at[most4], sems.at[1, 3])
    field = planes(recv_h)
    for j in range(SEG):
        head_out[0, pl.ds(j, SUB, stride=SEG), :] = field[8 * j : 8 * j + 8]

    wait_all(recv_o.at[most4], sems.at[1, 4])
    field = planes(recv_o)
    for j in range(SEG):
        tmp2[pl.ds(j, SUB, stride=SEG), :] = field[8 * j : 8 * j + 8]

    def body_brick(k, c):
        ty = (y + k) % NYD
        remote(
            tmp2.at[pl.ds(pl.multiple_of(16 * ty, 16), 16)],
            brick.at[y],
            sems.at[0, 5],
            sems.at[1, 5],
            (g, ty),
        ).start()
        return c

    lax.fori_loop(1, NYD, body_brick, 0)
    brick[y] = tmp2[pl.ds(pl.multiple_of(16 * y, 16), 16), :]
    wait_all(brick.at[pl.ds(0, NYD - 1)], sems.at[1, 5])
    for i in range(NYD):
        oxy_out[0, :, 128 * i : 128 * i + 128] = brick[i]

    halo(reg_a, 0, 2, (-1, 1, -2, 2), False)
    halo(reg_c, 1, 2, (-1, 1, -2, 2), False)
    halo(reg_d, 2, 1, (-1, 1), False)
    halo(reg_b, 3, 1, (-1, 1), False)
    wait_all(recv_a.at[most8], sems.at[0, 0])
    wait_all(recv_x.at[pl.ds(0, NX - 1)], sems.at[0, 1])
    wait_all(recv_b.at[most8], sems.at[0, 2])
    wait_all(recv_h.at[most4], sems.at[0, 3])
    wait_all(recv_o.at[most4], sems.at[0, 4])
    wait_all(brick.at[pl.ds(0, NYD - 1)], sems.at[0, 5])


def local(pressure_head, material_zone, emitters, oxygen, sulfide_rate, air_flux):
    vmem = pl.BlockSpec(memory_space=pltpu.VMEM)
    f32 = jnp.float32

    def buf(*shape):
        return pltpu.VMEM(shape, f32)

    block = (DEPTH, LANES)
    return pl.pallas_call(
        kernel,
        out_shape=(
            jax.ShapeDtypeStruct((1, DEPTH, LANES), f32),
            jax.ShapeDtypeStruct((1, DEPTH // NYD, LANES * NYD), f32),
        ),
        in_specs=[vmem] * 6,
        out_specs=(vmem, vmem),
        scratch_shapes=[
            buf(*block),
            buf(*block),
            buf(8 * NX, LANES),
            buf(8 * NX, LANES),
            buf(8 * NX, LANES),
            buf(8 * NX, LANES),
            buf(2, LANES),
            buf(NX, 2, LANES),
            buf(REGION, 264, LANES),
            buf(3, 256, LANES),
            buf(REGION, *block),
            buf(3, *block),
            buf(REGION, *block),
            buf(REGION, *block),
            buf(REGION, *block),
            buf(REGION, *block),
            buf(REGION, 5, *block),
            buf(REGION, 8 * NFAC, LANES),
            buf(2, REGION, *block),
            buf(3, *block),
            buf(2, 3, *block),
            buf(3, 3, *block),
            buf(3, 256, LANES),
            buf(NX, COLS, LANES),
            buf(NX, COLS, LANES),
            buf(NX, COLS, LANES),
            buf(NX, COLS, LANES),
            buf(NYD, DEPTH // NYD, LANES),
            pltpu.SemaphoreType.DMA((2, 6)),
            pltpu.SemaphoreType.DMA((4, REGION)),
            pltpu.SemaphoreType.DMA((4, REGION)),
        ],
        compiler_params=pltpu.CompilerParams(
            collective_id=0, has_side_effects=True, vmem_limit_bytes=32 * 1024 * 1024
        ),
    )(pressure_head, material_zone, emitters, oxygen, sulfide_rate, air_flux)


def solution(mesh):
    return jax.shard_map(
        local,
        mesh=mesh,
        in_specs=(
            P("gx", None, "gy"),
            P("gx", None, "gy"),
            P("gx", "gy"),
            P("gx", None, "gy"),
            P("gx", None, "gy"),
            P("gx", "gy"),
        ),
        out_specs=(P("gx", None, "gy"), P("gx", "gy", None)),
        check_vma=False,
    )
```

```python
import jax
import jax.numpy as jnp
from jax import lax
from jax.experimental import pallas as pl
from jax.experimental.pallas import tpu as pltpu
from jax.sharding import PartitionSpec as P

SWEEPS = 8
TABLE = (
    (4.0, 2.5, 1.2, 0.8),
    (2.4, 1.9, 1.6, 1.4),
    (0.05, 0.08, 0.1, 0.12),
    (0.38, 0.42, 0.45, 0.4),
    (5.0, 2.0, 0.6, 0.2),
)
FLOW_STEP = 2.0
STORAGE_TERM = 0.01
COND_FLOOR = 0.001
IRRIGATION = 0.3
GAS_STEP = 0.25

NX, NYD, LANES, DEPTH, SEG, SUB = 32, 8, 128, 128, 16, 8
COLS = LANES // NX
STRIPS = NX * NYD
REGION = 5
MESH = pl.DeviceIdType.MESH

FWD = 0
BACK = 30
SCALE = 60
LAST = 67
PREV = 75
NFAC = 83


def levels():
    result = []
    kept = list(range(SEG))
    place = 0
    scale = 0
    step = 1
    while len(kept) > 1:
        gone, stay = kept[0::2], kept[1::2]
        result.append((step, gone, stay, place, scale))
        place += len(gone)
        if step > 1:
            scale += len(gone)
        kept = stay
        step *= 2
    return result


LEVELS = levels()


def rows(j):
    return pl.ds(SUB * j, SUB)


def roll(x, shift, axis):
    return pltpu.roll(x, shift % x.shape[axis], axis)


def sel(masks, values):
    return jnp.where(
        masks[0],
        jnp.float32(values[0]),
        jnp.where(
            masks[1],
            jnp.float32(values[1]),
            jnp.where(masks[2], jnp.float32(values[2]), jnp.float32(values[3])),
        ),
    )


def zone_masks(zone):
    return (zone < 0.5, zone < 1.5, zone < 2.5)


def saturation(head, masks):
    a, n, r, s, k = TABLE
    au = sel(masks, a) * jnp.maximum(-head, 1e-37)
    power = jnp.exp2(sel(masks, [v - 1.0 for v in n]) * jnp.log2(au))
    one_p = 1.0 + power * au
    log_p = jnp.log2(one_p)
    m = sel(masks, [1.0 - 1.0 / v for v in n])
    return power, one_p, m * log_p


def harmonic(u, v):
    return 2.0 * u * v / (u + v)


def kernel(
    head_ref, zone_ref, em_ref, oxy_ref, sul_ref, flux_ref,
    head_out, oxy_out,
    tmp, tmp2, send_a, recv_a, send_b, recv_b, send_x, recv_x, reg_a, reg_b, reg_c, reg_d,
    cond, half_cap, se_old, raw, base, lat, face, row_a, row_c, fac, x, f,
    gas_g, gas_s, gas_f0, gas_f1, gas_c, gas_r,
    send_h, recv_h, send_o, recv_o, brick, in_h, in_z, in_o, in_s, in_e, in_f,
    sems, halo_s, halo_r, in_sem,
):
    g = lax.axis_index("gx")
    y = lax.axis_index("gy")

    def strip_of(gx):
        return gx + (gx // 16) * (47 - 2 * gx)

    s = strip_of(g)
    me = y * NX + s

    def device_of(strip):
        return (strip_of(strip % NX), strip // NX)

    lane = lax.broadcasted_iota(jnp.int32, (SUB, LANES), 1)
    sub = lax.broadcasted_iota(jnp.int32, (SUB, LANES), 0)
    plane = lane % NX
    col = lane // NX
    first_plane, last_plane = plane == 0, plane == NX - 1
    first_col, last_col = col == 0, col == COLS - 1
    top, bottom = sub == 0, sub == SUB - 1

    barrier = pltpu.get_barrier_semaphore()

    def greet_x(k, c):
        pl.semaphore_signal(barrier, inc=1, device_id=((g + k) % NX, y), device_id_type=MESH)
        return c

    def greet_y(k, c):
        pl.semaphore_signal(barrier, inc=1, device_id=(g, (y + k) % NYD), device_id_type=MESH)
        return c

    def valid(k):
        return jnp.logical_and(me + k >= 0, me + k < STRIPS)

    lax.fori_loop(1, NX, greet_x, 0, unroll=True)
    lax.fori_loop(1, NYD, greet_y, 0, unroll=True)
    for k in (-1, 1, -2, 2):
        @pl.when(jnp.logical_and(valid(k), jnp.logical_or(s + k < 0, s + k >= NX)))
        def _():
            pl.semaphore_signal(barrier, inc=1, device_id=device_of(me + k), device_id_type=MESH)

    loads = [
        pltpu.make_async_copy(src.at[0], dst, in_sem.at[i])
        for i, (src, dst) in enumerate(
            ((head_ref, in_h), (zone_ref, in_z), (oxy_ref, in_o), (sul_ref, in_s))
        )
    ]
    loads.append(pltpu.make_async_copy(em_ref, in_e, in_sem.at[4]))
    loads.append(pltpu.make_async_copy(flux_ref, in_f, in_sem.at[5]))
    for load in loads:
        load.start()

    def pack(first, second, out):
        for q in range(NX // 2):
            f = first[8 * q : 8 * q + 8]
            t = second[8 * q : 8 * q + 8]
            out[pl.ds(16 * q, 8), :] = jnp.where(sub < 4, f, roll(t, 4, 0))
            out[pl.ds(16 * q + 8, 8), :] = jnp.where(sub < 4, roll(f, 4, 0), t)

    def segmented(ref):
        return jnp.concatenate(
            [ref[pl.ds(j, SUB, stride=SEG), :].astype(jnp.float32) for j in range(SEG)], axis=0
        ).T

    loads[0].wait()
    loads[1].wait()
    pack(segmented(in_h), segmented(in_z), send_a)
    loads[4].wait()
    loads[5].wait()
    send_x[0:1, :] = in_e[...].astype(jnp.float32)
    send_x[1:2, :] = in_f[...]
    own = pl.ds(pl.multiple_of(8 * g, 8), 8)
    recv_a[own, :] = send_a[pl.ds(pl.multiple_of(8 * s, 8), 8), :]
    recv_x[g] = send_x[...]

    lower = (2 - jnp.minimum(s, 2)) * jnp.minimum(y, 1)
    upper = (2 - jnp.minimum(NX - 1 - s, 2)) * jnp.minimum(NYD - 1 - y, 1)
    pl.semaphore_wait(barrier, NX - 1 + NYD - 1 + lower + upper)

    def remote(src, dst, ssem, rsem, device):
        return pltpu.make_async_remote_copy(
            src_ref=src, dst_ref=dst, send_sem=ssem, recv_sem=rsem, device_id=device, device_id_type=MESH
        )

    def scatter8(src, dst, index):
        def body(k, c):
            tg = (g + k) % NX
            remote(
                src.at[pl.ds(pl.multiple_of(8 * strip_of(tg), 8), 8)],
                dst.at[pl.ds(pl.multiple_of(8 * g, 8), 8)],
                sems.at[0, index],
                sems.at[1, index],
                (tg, y),
            ).start()
            return c

        lax.fori_loop(1, NX, body, 0)

    def wait_all(part, sem):
        pltpu.make_async_copy(part, part, sem).wait()

    scatter8(send_a, recv_a, 0)

    def body_x(k, c):
        tg = (g + k) % NX
        remote(send_x, recv_x.at[g], sems.at[0, 1], sems.at[1, 1], (tg, y)).start()
        return c

    lax.fori_loop(1, NX, body_x, 0)

    loads[2].wait()
    loads[3].wait()
    pack(segmented(in_o), segmented(in_s), send_b)
    recv_b[own, :] = send_b[pl.ds(pl.multiple_of(8 * s, 8), 8), :]

    most8 = pl.ds(0, 8 * (NX - 1))
    wait_all(recv_a.at[most8], sems.at[1, 0])

    def unpack(src, field):
        parts = [
            src[pl.ds(64 * q + 4 * field + c, 8, stride=8), :] for c in range(COLS) for q in range(NX // 8)
        ]
        return jnp.concatenate(parts, axis=0).T

    reg_a[2, 0:128, :] = unpack(recv_a, 0)
    reg_a[2, 128:256, :] = unpack(recv_a, 1)
    wait_all(recv_x.at[pl.ds(0, NX - 1)], sems.at[1, 1])
    tmp[0:32, :] = recv_x[:, 0, :]
    tmp[32:64, :] = recv_x[:, 1, :]
    tmp[64:128, :] = jnp.zeros((64, LANES), jnp.float32)
    tmp2[...] = tmp[...].T
    emitted = jnp.zeros((1, LANES), jnp.float32)
    fluxes = jnp.zeros((1, LANES), jnp.float32)
    lane1 = lax.broadcasted_iota(jnp.int32, (1, LANES), 1) // NX
    for c in range(COLS):
        row = tmp2[pl.ds(4 * s + c, 1), :]
        emitted = jnp.where(lane1 == c, roll(row, 32 * c, 1), emitted)
        fluxes = jnp.where(lane1 == c, roll(row, 32 * c - 32, 1), fluxes)
    reg_a[2, 256:264, :] = jnp.concatenate(
        [emitted, fluxes, jnp.zeros((6, LANES), jnp.float32)], axis=0
    )

    def halo(reg, index, middle, ks, start):
        for k in ks:
            there = middle - k

            @pl.when(valid(k))
            def _():
                copy = remote(
                    reg.at[middle],
                    reg.at[there],
                    halo_s.at[index, middle + k],
                    halo_r.at[index, there],
                    device_of(me + k),
                )
                if start:
                    copy.start()
                else:
                    copy.wait_send()

    def arrive(reg, index, middle, b):
        strip = me + b - middle
        inside = jnp.logical_and(strip >= 0, strip < STRIPS)

        @pl.when(inside)
        def _():
            pltpu.make_async_copy(reg.at[b], reg.at[b], halo_r.at[index, b]).wait()

        @pl.when(jnp.logical_not(inside))
        def _():
            reg[b] = reg[middle]

    halo(reg_a, 0, 2, (-1, 1, -2, 2), True)
    scatter8(send_b, recv_b, 2)

    def picard(reg, index, first):
        def retain(i, carry):
            step = (i + 1) // 2
            b = 2 + step * (1 - 2 * (i % 2))

            @pl.when(i > 0)
            def _():
                arrive(reg, index, 2, b)

            for j in range(SEG):
                h = reg[b, rows(j), :]
                masks = zone_masks(reg_a[b, pl.ds(128 + 8 * j, 8), :])
                power, one_p, mlog = saturation(h, masks)
                se = jnp.exp2(-mlog)
                a, n, r, sat, kk = TABLE
                filled = power * se
                cap = (
                    sel(masks, [(w - v) * p * q * (1.0 - 1.0 / q) / FLOW_STEP for p, q, v, w in zip(a, n, r, sat)])
                    * filled
                    / one_p
                    + STORAGE_TERM / FLOW_STEP
                )
                rest = 1.0 - filled
                cond[b, rows(j), :] = sel(masks, kk) * (jnp.exp2(-0.5 * mlog) * rest * rest + COND_FLOOR)
                half_cap[b, rows(j), :] = cap
                x[b, rows(j), :] = h
                if first:
                    se_old[b, rows(j), :] = se
                    raw[b, rows(j), :] = cap * h
                else:
                    raw[b, rows(j), :] = cap * h - sel(
                        masks, [(w - v) / FLOW_STEP for v, w in zip(r, sat)]
                    ) * (se - se_old[b, rows(j), :])
            return carry

        lax.fori_loop(0, REGION, retain, 0)

        def right_faces(b, carry):
            after = jnp.minimum(b + 1, REGION - 1)
            strip = me + b - 2
            closed = jnp.logical_or(strip == -1, strip == STRIPS - 1)
            mask = jnp.where(last_col, jnp.where(closed, 0.0, 1.0), 1.0)
            for j in range(SEG):
                k = cond[b, rows(j), :]
                near = roll(jnp.where(first_col, cond[after, rows(j), :], k), -NX, 1)
                face[b, rows(j), :] = mask * harmonic(k, near)
            return carry

        lax.fori_loop(0, REGION, right_faces, 0)

        def assemble(b, carry):
            before = jnp.maximum(b - 1, 0)
            ks = [cond[b, rows(j), :] for j in range(SEG)]
            up0 = jnp.where(top, 0.0, harmonic(ks[0], roll(ks[SEG - 1], 1, 0)))
            ups = [up0] + [harmonic(ks[j], ks[j - 1]) for j in range(1, SEG)]
            los = ups[1:] + [roll(up0, -1, 0)]
            for j in range(SEG):
                k = ks[j]
                xp = jnp.where(last_plane, 0.0, harmonic(k, roll(k, -1, 1)))
                xm = roll(xp, 1, 1)
                yp = face[b, rows(j), :]
                ym = roll(jnp.where(last_col, face[before, rows(j), :], yp), NX, 1)
                diag = half_cap[b, rows(j), :] + xp + xm + yp + ym + ups[j] + los[j]
                inv = 1.0 / diag
                rhs = raw[b, rows(j), :] + ups[j] - los[j]
                if j == SEG - 1:
                    rhs = rhs - jnp.where(bottom, k, 0.0)
                if j == 0:
                    rhs = rhs + jnp.where(top, IRRIGATION * reg_a[b, pl.ds(256, 1), :], 0.0)
                base[b, rows(j), :] = rhs * inv
                lat[b, rows(j), :] = xm * inv
                lat[b, rows(SEG + j), :] = xp * inv
                lat[b, rows(2 * SEG + j), :] = ym * inv
                lat[b, rows(3 * SEG + j), :] = yp * inv
                row_a[b, rows(j), :] = ups[j] * inv
                row_c[b, rows(j), :] = los[j] * inv
            return carry

        lax.fori_loop(0, REGION, assemble, 0)

        def factor(blocks):
            state = {}
            for b in blocks:
                state[b] = (
                    [row_a[b, rows(j), :] for j in range(SEG)],
                    [None] * SEG,
                    [row_c[b, rows(j), :] for j in range(SEG)],
                )

            def put(b, i, value):
                fac[b, rows(i), :] = value

            for step, gone, stay, place, scale in LEVELS:
                for b in blocks:
                    av, bv, cv = state[b]
                    for i, e in enumerate(gone):
                        if step > 1:
                            bv[e] = 1.0 / bv[e]
                            put(b, SCALE + scale + i, bv[e])
                            av[e] = av[e] * bv[e]
                            cv[e] = cv[e] * bv[e]
                        put(b, BACK + place + i, av[e])
                        put(b, BACK + 15 + place + i, cv[e])
                for b in blocks:
                    av, bv, cv = state[b]
                    new = {}
                    for i, j in enumerate(stay):
                        up, dn = j - step, j + step
                        wrap = dn >= SEG
                        dn = dn % SEG
                        a_dn, c_dn = av[dn], cv[dn]
                        alpha, gamma = av[j], cv[j]
                        if step > 1:
                            alpha = alpha * bv[up]
                        if wrap:
                            a_dn, c_dn = roll(a_dn, -1, 0), roll(c_dn, -1, 0)
                            gamma = roll(gamma, 1, 0)
                        if step > 1:
                            gamma = gamma * bv[dn]
                        diag = (bv[j] if step > 1 else 1.0) - av[j] * cv[up] - cv[j] * a_dn
                        put(b, FWD + place + i, alpha)
                        put(b, FWD + 15 + place + i, gamma)
                        new[j] = (av[j] * av[up], diag, cv[j] * c_dn)
                    for j in stay:
                        av[j], bv[j], cv[j] = new[j]
            last = {b: (v[0][SEG - 1], v[1][SEG - 1], v[2][SEG - 1]) for b, v in state.items()}
            multipliers = {b: [] for b in blocks}
            for step in (1, 2, 4):
                for b in blocks:
                    a, d, c = last[b]
                    inv = 1.0 / d
                    alpha = a * roll(inv, step, 0)
                    gamma = c * roll(inv, -step, 0)
                    multipliers[b].append((alpha, gamma))
                    d = d - alpha * roll(c, step, 0) - gamma * roll(a, -step, 0)
                    last[b] = (alpha * roll(a, step, 0), d, gamma * roll(c, -step, 0))
            for b in blocks:
                (a1, g1), (a2, g2), (a4, g4) = multipliers[b]
                beta = a4 + g4
                inv = 1.0 / last[b][1]
                diags = [
                    None,
                    a1 + a2 * roll(g1, 2, 0),
                    a2,
                    a2 * roll(a1, 2, 0),
                    None,
                    g2 * roll(g1, -2, 0),
                    g2,
                    g1 + g2 * roll(a1, -2, 0),
                ]
                final = []
                for k in range(SUB):
                    if k == 0:
                        value = inv
                    elif k == 4:
                        value = inv * beta
                    else:
                        value = inv * (diags[k] + beta * roll(diags[(k + 4) % 8], 4, 0))
                    put(b, LAST + k, value)
                    put(b, PREV + (k + 1) % 8, roll(value, 1, 0))

        factor((0, 1, 2))
        factor((3, 4))

        def sources(b):
            before, after = max(b - 1, 0), min(b + 1, REGION - 1)
            for j in range(SEG):
                v = x[b, rows(j), :]
                left = jnp.where(last_col, x[before, rows(j), :], v)
                right = jnp.where(first_col, x[after, rows(j), :], v)
                f[b, rows(j), :] = (
                    base[b, rows(j), :]
                    + lat[b, rows(j), :] * roll(v, 1, 1)
                    + lat[b, rows(SEG + j), :] * roll(v, -1, 1)
                    + lat[b, rows(2 * SEG + j), :] * roll(left, NX, 1)
                    + lat[b, rows(3 * SEG + j), :] * roll(right, -NX, 1)
                )

        def solve(blocks):
            def get(b, i):
                return fac[b, rows(i), :]

            values = {b: [f[b, rows(j), :] for j in range(SEG)] for b in blocks}
            wrapped = {b: None for b in blocks}
            for step, gone, stay, place, scale in LEVELS:
                for b in blocks:
                    v = values[b]
                    for i, j in enumerate(stay):
                        v[j] = v[j] + get(b, FWD + place + i) * v[j - step]
                        gamma = get(b, FWD + 15 + place + i)
                        if j + step < SEG:
                            v[j] = v[j] + gamma * v[j + step]
                        elif step == 1:
                            wrapped[b] = gamma * v[0]
                        else:
                            wrapped[b] = wrapped[b] + gamma * v[j + step - SEG]
            lasts = {}
            for b in blocks:
                lasts[b] = values[b][SEG - 1] + roll(wrapped[b], -1, 0)
            above = {}
            for b in blocks:
                turned = [lasts[b]] + [roll(lasts[b], k, 0) for k in range(1, SUB)]
                here = [get(b, LAST + k) * turned[k] for k in range(SUB)]
                prev = [get(b, PREV + k) * turned[k] for k in range(SUB)]
                while len(here) > 1:
                    here = [p + q for p, q in zip(here[0::2], here[1::2])]
                    prev = [p + q for p, q in zip(prev[0::2], prev[1::2])]
                values[b][SEG - 1] = here[0]
                above[b] = prev[0]
            for step, gone, stay, place, scale in reversed(LEVELS):
                for b in blocks:
                    v = values[b]
                    for i, e in enumerate(gone):
                        up = v[e - step] if e >= step else above[b]
                        src = v[e] * get(b, SCALE + scale + i) if step > 1 else v[e]
                        v[e] = src + get(b, BACK + place + i) * up + get(b, BACK + 15 + place + i) * v[e + step]
            for b in blocks:
                for j in range(SEG):
                    x[b, rows(j), :] = values[b][j]

        def relax(groups):
            def body(t, carry):
                for group in groups:
                    for b in group:
                        sources(b)
                for group in groups:
                    solve(group)
                return carry

            return body

        lax.fori_loop(0, 3, relax(((0, 1, 2), (3, 4))), 0)
        lax.fori_loop(3, 7, relax(((1, 2, 3),)), 0)
        relax(((2,),))(7, 0)

    picard(reg_a, 0, True)
    reg_c[2] = x[2]
    halo(reg_c, 1, 2, (-1, 1, -2, 2), True)

    wait_all(recv_b.at[most8], sems.at[1, 2])
    reg_b[1, 0:128, :] = unpack(recv_b, 0)
    reg_b[1, 128:256, :] = unpack(recv_b, 1)
    halo(reg_b, 3, 1, (-1, 1), True)

    picard(reg_c, 1, False)
    reg_d[1] = x[2]
    halo(reg_d, 2, 1, (-1, 1), True)

    def scatter4(src, dst, index):
        def body(k, c):
            tg = (g + k) % NX
            remote(src.at[tg], dst.at[s], sems.at[0, index], sems.at[1, index], (tg, y)).start()
            return c

        lax.fori_loop(1, NX, body, 0)

    def pack_planes(field, out, own_slot):
        tmp[...] = field.T
        for p in range(NX):
            out[p] = tmp[pl.ds(p, COLS, stride=NX), :]
        own_slot[s] = out[g]

    pack_planes(x[2], send_h, recv_h)
    scatter4(send_h, recv_h, 3)

    def gas_prepare(i, carry):
        b = (i + 1) % 3

        @pl.when(i > 0)
        def _():
            arrive(reg_b, 3, 1, b)
            arrive(reg_d, 2, 1, b)

        strip = me + b - 1
        inside = jnp.where(jnp.logical_and(strip >= 0, strip < STRIPS), 1.0, 0.0)
        a, n, r, sat, kk = TABLE
        for j in range(SEG):
            masks = zone_masks(reg_a[b + 1, pl.ds(128 + 8 * j, 8), :])
            power, one_p, mlog = saturation(reg_d[b, rows(j), :], masks)
            se = jnp.exp2(-mlog)
            span = sel(masks, [w - v for v, w in zip(r, sat)])
            inv_s = sel(masks, [1.0 / w for w in sat])
            gas = jnp.maximum(span * (1.0 - se), 1e-37)
            root = jnp.exp2((5.0 / 3.0) * jnp.log2(gas)) * inv_s * inside
            conc = reg_b[b, rows(j), :]
            gas_g[b, rows(j), :] = root
            gas_f0[b, rows(j), :] = root * conc
            gas_r[b, rows(j), :] = reg_b[b, pl.ds(128 + 8 * j, 8), :] * (sel(masks, r) + span * se) * inv_s
            gas_r[b, pl.ds(128 + 8 * j, 8), :] = GAS_STEP * inv_s
        return carry

    lax.fori_loop(0, 3, gas_prepare, 0)

    def around(ref, b, j):
        before, after = max(b - 1, 0), min(b + 1, 2)
        v = ref[b, rows(j), :]
        left = jnp.where(last_col, ref[before, rows(j), :], v)
        right = jnp.where(first_col, ref[after, rows(j), :], v)
        above = ref[b, rows(j - 1), :] if j > 0 else jnp.where(top, 0.0, roll(ref[b, rows(SEG - 1), :], 1, 0))
        below = ref[b, rows(j + 1), :] if j < SEG - 1 else jnp.where(bottom, 0.0, roll(ref[b, rows(0), :], -1, 0))
        return (
            jnp.where(first_plane, 0.0, roll(v, 1, 1))
            + jnp.where(last_plane, 0.0, roll(v, -1, 1))
            + roll(left, NX, 1)
            + roll(right, -NX, 1)
            + above
            + below
        )

    def gas_advance(b, old, flow, store):
        flux = reg_a[b + 1, pl.ds(257, 1), :]
        for j in range(SEG):
            conc = old[b, rows(j), :]
            root = gas_g[b, rows(j), :]
            if j < SEG - 1:
                under = old[b, rows(j + 1), :]
            else:
                under = jnp.where(bottom, 1.0, roll(old[b, rows(0), :], -1, 0))
            change = (
                root * (around(flow, b, j) - conc * gas_s[b, rows(j), :])
                + flux * (under - conc)
                - gas_r[b, rows(j), :] * conc
            )
            if j == 0:
                change = change + jnp.where(top, 2.0 * root * root * (1.0 - conc), 0.0)
            store(j, conc + gas_r[b, pl.ds(128 + 8 * j, 8), :] * change, root)

    for b in range(3):

        def first_store(j, new, root, b=b):
            gas_c[b, rows(j), :] = new
            gas_f1[b, rows(j), :] = root * new

        for j in range(SEG):
            gas_s[b, rows(j), :] = around(gas_g, b, j)
        gas_advance(b, reg_b, gas_f0, first_store)

    def second_store(j, new, root):
        tmp2[rows(j), :] = new

    gas_advance(1, gas_c, gas_f1, second_store)

    pack_planes(tmp2[...], send_o, recv_o)
    scatter4(send_o, recv_o, 4)

    def planes(src):
        return jnp.concatenate([src[i] for i in range(NX)], axis=0).T

    most4 = pl.ds(0, NX - 1)
    wait_all(recv_h.at[most4], sems.at[1, 3])
    field = planes(recv_h)
    for j in range(SEG):
        head_out[0, pl.ds(j, SUB, stride=SEG), :] = field[8 * j : 8 * j + 8]

    wait_all(recv_o.at[most4], sems.at[1, 4])
    field = planes(recv_o)
    for j in range(SEG):
        tmp2[pl.ds(j, SUB, stride=SEG), :] = field[8 * j : 8 * j + 8]

    def body_brick(k, c):
        ty = (y + k) % NYD
        remote(
            tmp2.at[pl.ds(pl.multiple_of(16 * ty, 16), 16)],
            brick.at[y],
            sems.at[0, 5],
            sems.at[1, 5],
            (g, ty),
        ).start()
        return c

    lax.fori_loop(1, NYD, body_brick, 0)
    brick[y] = tmp2[pl.ds(pl.multiple_of(16 * y, 16), 16), :]
    wait_all(brick.at[pl.ds(0, NYD - 1)], sems.at[1, 5])
    for i in range(NYD):
        oxy_out[0, :, 128 * i : 128 * i + 128] = brick[i]

    halo(reg_a, 0, 2, (-1, 1, -2, 2), False)
    halo(reg_c, 1, 2, (-1, 1, -2, 2), False)
    halo(reg_d, 2, 1, (-1, 1), False)
    halo(reg_b, 3, 1, (-1, 1), False)
    wait_all(recv_a.at[most8], sems.at[0, 0])
    wait_all(recv_x.at[pl.ds(0, NX - 1)], sems.at[0, 1])
    wait_all(recv_b.at[most8], sems.at[0, 2])
    wait_all(recv_h.at[most4], sems.at[0, 3])
    wait_all(recv_o.at[most4], sems.at[0, 4])
    wait_all(brick.at[pl.ds(0, NYD - 1)], sems.at[0, 5])


def local(pressure_head, material_zone, emitters, oxygen, sulfide_rate, air_flux):
    vmem = pl.BlockSpec(memory_space=pltpu.VMEM)
    f32 = jnp.float32

    def buf(*shape):
        return pltpu.VMEM(shape, f32)

    block = (DEPTH, LANES)
    done = pl.pallas_call(
        kernel,
        out_shape=(
            jax.ShapeDtypeStruct((1, DEPTH, LANES), f32),
            jax.ShapeDtypeStruct((1, DEPTH // NYD, LANES * NYD), f32),
        ),
        in_specs=[pl.BlockSpec(memory_space=pl.ANY)] * 6,
        out_specs=(vmem, vmem),
        scratch_shapes=[
            buf(*block),
            buf(*block),
            buf(8 * NX, LANES),
            buf(8 * NX, LANES),
            buf(8 * NX, LANES),
            buf(8 * NX, LANES),
            buf(2, LANES),
            buf(NX, 2, LANES),
            buf(REGION, 264, LANES),
            buf(3, 256, LANES),
            buf(REGION, *block),
            buf(3, *block),
            buf(REGION, *block),
            buf(REGION, *block),
            buf(REGION, *block),
            buf(REGION, *block),
            buf(REGION, *block),
            buf(REGION, 4 * DEPTH, LANES),
            buf(REGION, *block),
            buf(REGION, *block),
            buf(REGION, *block),
            buf(REGION, 8 * NFAC, LANES),
            buf(REGION, *block),
            buf(REGION, *block),
            buf(3, *block),
            buf(3, *block),
            buf(3, *block),
            buf(3, *block),
            buf(3, *block),
            buf(3, 256, LANES),
            buf(NX, COLS, LANES),
            buf(NX, COLS, LANES),
            buf(NX, COLS, LANES),
            buf(NX, COLS, LANES),
            buf(NYD, DEPTH // NYD, LANES),
            buf(*block),
            pltpu.VMEM(block, jnp.int32),
            buf(*block),
            buf(*block),
            pltpu.VMEM((1, LANES), jnp.int32),
            buf(1, LANES),
            pltpu.SemaphoreType.DMA((2, 6)),
            pltpu.SemaphoreType.DMA((4, REGION)),
            pltpu.SemaphoreType.DMA((4, REGION)),
            pltpu.SemaphoreType.DMA((6,)),
        ],
        compiler_params=pltpu.CompilerParams(
            collective_id=0, has_side_effects=True, vmem_limit_bytes=64 * 1024 * 1024
        ),
    )(pressure_head, material_zone, emitters, oxygen, sulfide_rate, air_flux)
    return pl.pallas_call(
        finish,
        out_shape=tuple(jax.ShapeDtypeStruct(v.shape, f32) for v in done),
        in_specs=[vmem] * 2,
        out_specs=(vmem, vmem),
    )(*done)


def finish(head, oxygen, head_out, oxygen_out):
    head_out[...] = head[...]
    oxygen_out[...] = oxygen[...]


def solution(mesh):
    return jax.shard_map(
        local,
        mesh=mesh,
        in_specs=(
            P("gx", None, "gy"),
            P("gx", None, "gy"),
            P("gx", "gy"),
            P("gx", None, "gy"),
            P("gx", None, "gy"),
            P("gx", "gy"),
        ),
        out_specs=(P("gx", None, "gy"), P("gx", "gy", None)),
        check_vma=False,
    )
```

```python
import jax
import jax.numpy as jnp
from jax import lax
from jax.experimental import pallas as pl
from jax.experimental.pallas import tpu as pltpu
from jax.sharding import PartitionSpec as P

SWEEPS = 8
TABLE = (
    (4.0, 2.5, 1.2, 0.8),
    (2.4, 1.9, 1.6, 1.4),
    (0.05, 0.08, 0.1, 0.12),
    (0.38, 0.42, 0.45, 0.4),
    (5.0, 2.0, 0.6, 0.2),
)
FLOW_STEP = 2.0
STORAGE_TERM = 0.01
COND_FLOOR = 0.001
IRRIGATION = 0.3
GAS_STEP = 0.25

NX, NYD, LANES, DEPTH, SEG, SUB = 32, 8, 128, 128, 16, 8
COLS = LANES // NX
STRIPS = NX * NYD
REGION = 5
MESH = pl.DeviceIdType.MESH

FWD = 0
BACK = 30
SCALE = 60
LAST = 67
PREV = 75
NFAC = 83


def levels():
    result = []
    kept = list(range(SEG))
    place = 0
    scale = 0
    step = 1
    while len(kept) > 1:
        gone, stay = kept[0::2], kept[1::2]
        result.append((step, gone, stay, place, scale))
        place += len(gone)
        if step > 1:
            scale += len(gone)
        kept = stay
        step *= 2
    return result


LEVELS = levels()


def rows(j):
    return pl.ds(SUB * j, SUB)


def roll(x, shift, axis):
    return pltpu.roll(x, shift % x.shape[axis], axis)


def sel(masks, values):
    return jnp.where(
        masks[0],
        jnp.float32(values[0]),
        jnp.where(
            masks[1],
            jnp.float32(values[1]),
            jnp.where(masks[2], jnp.float32(values[2]), jnp.float32(values[3])),
        ),
    )


def zone_masks(zone):
    return (zone < 0.5, zone < 1.5, zone < 2.5)


def saturation(head, masks):
    a, n, r, s, k = TABLE
    au = sel(masks, a) * jnp.maximum(-head, 1e-37)
    power = jnp.exp2(sel(masks, [v - 1.0 for v in n]) * jnp.log2(au))
    one_p = 1.0 + power * au
    log_p = jnp.log2(one_p)
    m = sel(masks, [1.0 - 1.0 / v for v in n])
    return power, one_p, m * log_p


def harmonic(u, v):
    return 2.0 * u * v / (u + v)


def kernel(
    head_ref, zone_ref, em_ref, oxy_ref, sul_ref, flux_ref,
    head_out, oxy_out,
    tmp, tmp2, send_a, recv_a, send_b, recv_b, send_x, recv_x, reg_a, reg_x, reg_b, reg_c, reg_d,
    cond, half_cap, se_old, raw, base, lat, face, row_a, row_c, fac, x, f,
    gas_g, gas_s, gas_f0, gas_f1, gas_c, gas_r,
    send_h, recv_h, send_o, recv_o, brick, in_h, in_z, in_o, in_s, in_e, in_f,
    sems, halo_s, halo_r, in_sem,
):
    g = lax.axis_index("gx")
    y = lax.axis_index("gy")

    def strip_of(gx):
        return gx + (gx // 16) * (47 - 2 * gx)

    s = strip_of(g)
    me = y * NX + s

    def device_of(strip):
        return (strip_of(strip % NX), strip // NX)

    lane = lax.broadcasted_iota(jnp.int32, (SUB, LANES), 1)
    sub = lax.broadcasted_iota(jnp.int32, (SUB, LANES), 0)
    plane = lane % NX
    col = lane // NX
    first_plane, last_plane = plane == 0, plane == NX - 1
    first_col, last_col = col == 0, col == COLS - 1
    top, bottom = sub == 0, sub == SUB - 1

    half, ring, core = g // 16, (g // 2) % 8, g % 2
    partners = [
        ((half + dh) % 2) * 16 + ((ring + dz) % 8) * 2 + (core + dc) % 2
        for dh, dz, dc in sorted(
            ((dh, dz, dc) for dh in range(2) for dz in range(8) for dc in range(2)),
            key=lambda d: (-(2 * d[0] + min(d[1], 8 - d[1])), d),
        )
        if (dh, dz, dc) != (0, 0, 0)
    ]

    barrier = pltpu.get_barrier_semaphore()

    def greet_y(k, c):
        pl.semaphore_signal(barrier, inc=1, device_id=(g, (y + k) % NYD), device_id_type=MESH)
        return c

    def valid(k):
        return jnp.logical_and(me + k >= 0, me + k < STRIPS)

    for tg in partners:
        pl.semaphore_signal(barrier, inc=1, device_id=(tg, y), device_id_type=MESH)
    lax.fori_loop(1, NYD, greet_y, 0, unroll=True)
    for k in (-1, 1, -2, 2):
        @pl.when(jnp.logical_and(valid(k), jnp.logical_or(s + k < 0, s + k >= NX)))
        def _():
            pl.semaphore_signal(barrier, inc=1, device_id=device_of(me + k), device_id_type=MESH)

    loads = [
        pltpu.make_async_copy(src.at[0], dst, in_sem.at[i])
        for i, (src, dst) in enumerate(
            ((head_ref, in_h), (zone_ref, in_z), (oxy_ref, in_o), (sul_ref, in_s))
        )
    ]
    loads.append(pltpu.make_async_copy(em_ref, in_e, in_sem.at[4]))
    loads.append(pltpu.make_async_copy(flux_ref, in_f, in_sem.at[5]))
    for load in loads:
        load.start()

    def pack(first, second, out):
        for q in range(NX // 2):
            f = first[8 * q : 8 * q + 8]
            t = second[8 * q : 8 * q + 8]
            out[pl.ds(16 * q, 8), :] = jnp.where(sub < 4, f, roll(t, 4, 0))
            out[pl.ds(16 * q + 8, 8), :] = jnp.where(sub < 4, roll(f, 4, 0), t)

    def segmented(ref):
        return jnp.concatenate(
            [ref[pl.ds(j, SUB, stride=SEG), :].astype(jnp.float32) for j in range(SEG)], axis=0
        ).T

    loads[0].wait()
    loads[1].wait()
    pack(segmented(in_h), segmented(in_z), send_a)
    loads[4].wait()
    loads[5].wait()
    send_x[0:1, :] = in_e[...].astype(jnp.float32)
    send_x[1:2, :] = in_f[...]
    own = pl.ds(pl.multiple_of(8 * g, 8), 8)
    recv_a[own, :] = send_a[pl.ds(pl.multiple_of(8 * s, 8), 8), :]
    recv_x[g] = send_x[...]

    lower = (2 - jnp.minimum(s, 2)) * jnp.minimum(y, 1)
    upper = (2 - jnp.minimum(NX - 1 - s, 2)) * jnp.minimum(NYD - 1 - y, 1)
    pl.semaphore_wait(barrier, NX - 1 + NYD - 1 + lower + upper)

    def remote(src, dst, ssem, rsem, device):
        return pltpu.make_async_remote_copy(
            src_ref=src, dst_ref=dst, send_sem=ssem, recv_sem=rsem, device_id=device, device_id_type=MESH
        )

    def scatter8(src, dst, index):
        for tg in partners:
            remote(
                src.at[pl.ds(pl.multiple_of(8 * strip_of(tg), 8), 8)],
                dst.at[pl.ds(pl.multiple_of(8 * g, 8), 8)],
                sems.at[0, index],
                sems.at[1, index],
                (tg, y),
            ).start()

    def wait_all(part, sem):
        pltpu.make_async_copy(part, part, sem).wait()

    scatter8(send_a, recv_a, 0)

    for tg in partners:
        remote(send_x, recv_x.at[g], sems.at[0, 1], sems.at[1, 1], (tg, y)).start()

    loads[2].wait()
    loads[3].wait()
    pack(segmented(in_o), segmented(in_s), send_b)
    recv_b[own, :] = send_b[pl.ds(pl.multiple_of(8 * s, 8), 8), :]

    most8 = pl.ds(0, 8 * (NX - 1))
    wait_all(recv_a.at[most8], sems.at[1, 0])

    def unpack(src, field):
        parts = [
            src[pl.ds(64 * q + 4 * field + c, 8, stride=8), :] for c in range(COLS) for q in range(NX // 8)
        ]
        return jnp.concatenate(parts, axis=0).T

    reg_a[2, 0:128, :] = unpack(recv_a, 0)
    reg_a[2, 128:256, :] = unpack(recv_a, 1)
    def halo(reg, index, middle, ks, start):
        for k in ks:
            there = middle - k

            @pl.when(valid(k))
            def _():
                copy = remote(
                    reg.at[middle],
                    reg.at[there],
                    halo_s.at[index, middle + k],
                    halo_r.at[index, there],
                    device_of(me + k),
                )
                if start:
                    copy.start()
                else:
                    copy.wait_send()

    def arrive(reg, index, middle, b):
        strip = me + b - middle
        inside = jnp.logical_and(strip >= 0, strip < STRIPS)

        @pl.when(inside)
        def _():
            pltpu.make_async_copy(reg.at[b], reg.at[b], halo_r.at[index, b]).wait()

        @pl.when(jnp.logical_not(inside))
        def _():
            reg[b] = reg[middle]

    halo(reg_a, 0, 2, (-1, 1, -2, 2), True)
    wait_all(recv_x.at[pl.ds(0, NX - 1)], sems.at[1, 1])
    tmp[0:32, :] = recv_x[:, 0, :]
    tmp[32:64, :] = recv_x[:, 1, :]
    tmp[64:128, :] = jnp.zeros((64, LANES), jnp.float32)
    tmp2[...] = tmp[...].T
    emitted = jnp.zeros((1, LANES), jnp.float32)
    fluxes = jnp.zeros((1, LANES), jnp.float32)
    lane1 = lax.broadcasted_iota(jnp.int32, (1, LANES), 1) // NX
    for c in range(COLS):
        row = tmp2[pl.ds(4 * s + c, 1), :]
        emitted = jnp.where(lane1 == c, roll(row, 32 * c, 1), emitted)
        fluxes = jnp.where(lane1 == c, roll(row, 32 * c - 32, 1), fluxes)
    reg_x[2] = jnp.concatenate(
        [emitted, fluxes, jnp.zeros((6, LANES), jnp.float32)], axis=0
    )

    halo(reg_x, 4, 2, (-1, 1, -2, 2), True)

    def picard(reg, index, first, meanwhile):
        def retain(i, carry):
            step = (i + 1) // 2
            b = 2 + step * (1 - 2 * (i % 2))

            @pl.when(i > 0)
            def _():
                arrive(reg, index, 2, b)

            for j in range(SEG):
                h = reg[b, rows(j), :]
                masks = zone_masks(reg_a[b, pl.ds(128 + 8 * j, 8), :])
                power, one_p, mlog = saturation(h, masks)
                se = jnp.exp2(-mlog)
                a, n, r, sat, kk = TABLE
                filled = power * se
                cap = (
                    sel(masks, [(w - v) * p * q * (1.0 - 1.0 / q) / FLOW_STEP for p, q, v, w in zip(a, n, r, sat)])
                    * filled
                    / one_p
                    + STORAGE_TERM / FLOW_STEP
                )
                rest = 1.0 - filled
                cond[b, rows(j), :] = sel(masks, kk) * (jnp.exp2(-0.5 * mlog) * rest * rest + COND_FLOOR)
                half_cap[b, rows(j), :] = cap
                x[b, rows(j), :] = h
                if first:
                    se_old[b, rows(j), :] = se
                    raw[b, rows(j), :] = cap * h
                else:
                    raw[b, rows(j), :] = cap * h - sel(
                        masks, [(w - v) / FLOW_STEP for v, w in zip(r, sat)]
                    ) * (se - se_old[b, rows(j), :])
            return carry

        lax.fori_loop(0, REGION, retain, 0)
        meanwhile()

        def right_faces(b, carry):
            after = jnp.minimum(b + 1, REGION - 1)
            strip = me + b - 2
            closed = jnp.logical_or(strip == -1, strip == STRIPS - 1)
            mask = jnp.where(last_col, jnp.where(closed, 0.0, 1.0), 1.0)
            for j in range(SEG):
                k = cond[b, rows(j), :]
                near = roll(jnp.where(first_col, cond[after, rows(j), :], k), -NX, 1)
                face[b, rows(j), :] = mask * harmonic(k, near)
            return carry

        lax.fori_loop(0, REGION, right_faces, 0)

        def assemble(b, carry):
            before = jnp.maximum(b - 1, 0)
            ks = [cond[b, rows(j), :] for j in range(SEG)]
            up0 = jnp.where(top, 0.0, harmonic(ks[0], roll(ks[SEG - 1], 1, 0)))
            ups = [up0] + [harmonic(ks[j], ks[j - 1]) for j in range(1, SEG)]
            los = ups[1:] + [roll(up0, -1, 0)]
            for j in range(SEG):
                k = ks[j]
                xp = jnp.where(last_plane, 0.0, harmonic(k, roll(k, -1, 1)))
                xm = roll(xp, 1, 1)
                yp = face[b, rows(j), :]
                ym = roll(jnp.where(last_col, face[before, rows(j), :], yp), NX, 1)
                diag = half_cap[b, rows(j), :] + xp + xm + yp + ym + ups[j] + los[j]
                inv = 1.0 / diag
                rhs = raw[b, rows(j), :] + ups[j] - los[j]
                if j == SEG - 1:
                    rhs = rhs - jnp.where(bottom, k, 0.0)
                if j == 0:
                    rhs = rhs + jnp.where(top, IRRIGATION * reg_x[b, pl.ds(0, 1), :], 0.0)
                base[b, rows(j), :] = rhs * inv
                lat[b, rows(j), :] = xm * inv
                lat[b, rows(SEG + j), :] = xp * inv
                lat[b, rows(2 * SEG + j), :] = ym * inv
                lat[b, rows(3 * SEG + j), :] = yp * inv
                row_a[b, rows(j), :] = ups[j] * inv
                row_c[b, rows(j), :] = los[j] * inv
            return carry

        lax.fori_loop(0, REGION, assemble, 0)

        def factor(blocks):
            state = {}
            for b in blocks:
                state[b] = (
                    [row_a[b, rows(j), :] for j in range(SEG)],
                    [None] * SEG,
                    [row_c[b, rows(j), :] for j in range(SEG)],
                )

            def put(b, i, value):
                fac[b, rows(i), :] = value

            for step, gone, stay, place, scale in LEVELS:
                for b in blocks:
                    av, bv, cv = state[b]
                    for i, e in enumerate(gone):
                        if step > 1:
                            bv[e] = 1.0 / bv[e]
                            put(b, SCALE + scale + i, bv[e])
                            av[e] = av[e] * bv[e]
                            cv[e] = cv[e] * bv[e]
                        put(b, BACK + place + i, av[e])
                        put(b, BACK + 15 + place + i, cv[e])
                for b in blocks:
                    av, bv, cv = state[b]
                    new = {}
                    for i, j in enumerate(stay):
                        up, dn = j - step, j + step
                        wrap = dn >= SEG
                        dn = dn % SEG
                        a_dn, c_dn = av[dn], cv[dn]
                        alpha, gamma = av[j], cv[j]
                        if step > 1:
                            alpha = alpha * bv[up]
                        if wrap:
                            a_dn, c_dn = roll(a_dn, -1, 0), roll(c_dn, -1, 0)
                            gamma = roll(gamma, 1, 0)
                        if step > 1:
                            gamma = gamma * bv[dn]
                        diag = (bv[j] if step > 1 else 1.0) - av[j] * cv[up] - cv[j] * a_dn
                        put(b, FWD + place + i, alpha)
                        put(b, FWD + 15 + place + i, gamma)
                        new[j] = (av[j] * av[up], diag, cv[j] * c_dn)
                    for j in stay:
                        av[j], bv[j], cv[j] = new[j]
            last = {b: (v[0][SEG - 1], v[1][SEG - 1], v[2][SEG - 1]) for b, v in state.items()}
            multipliers = {b: [] for b in blocks}
            for step in (1, 2, 4):
                for b in blocks:
                    a, d, c = last[b]
                    inv = 1.0 / d
                    alpha = a * roll(inv, step, 0)
                    gamma = c * roll(inv, -step, 0)
                    multipliers[b].append((alpha, gamma))
                    d = d - alpha * roll(c, step, 0) - gamma * roll(a, -step, 0)
                    last[b] = (alpha * roll(a, step, 0), d, gamma * roll(c, -step, 0))
            for b in blocks:
                (a1, g1), (a2, g2), (a4, g4) = multipliers[b]
                beta = a4 + g4
                inv = 1.0 / last[b][1]
                diags = [
                    None,
                    a1 + a2 * roll(g1, 2, 0),
                    a2,
                    a2 * roll(a1, 2, 0),
                    None,
                    g2 * roll(g1, -2, 0),
                    g2,
                    g1 + g2 * roll(a1, -2, 0),
                ]
                final = []
                for k in range(SUB):
                    if k == 0:
                        value = inv
                    elif k == 4:
                        value = inv * beta
                    else:
                        value = inv * (diags[k] + beta * roll(diags[(k + 4) % 8], 4, 0))
                    put(b, LAST + k, value)
                    put(b, PREV + (k + 1) % 8, roll(value, 1, 0))

        factor((0, 1, 2))
        factor((3, 4))

        def sources(b):
            before, after = max(b - 1, 0), min(b + 1, REGION - 1)
            for j in range(SEG):
                v = x[b, rows(j), :]
                left = jnp.where(last_col, x[before, rows(j), :], v)
                right = jnp.where(first_col, x[after, rows(j), :], v)
                f[b, rows(j), :] = (
                    base[b, rows(j), :]
                    + lat[b, rows(j), :] * roll(v, 1, 1)
                    + lat[b, rows(SEG + j), :] * roll(v, -1, 1)
                    + lat[b, rows(2 * SEG + j), :] * roll(left, NX, 1)
                    + lat[b, rows(3 * SEG + j), :] * roll(right, -NX, 1)
                )

        def solve(blocks):
            def get(b, i):
                return fac[b, rows(i), :]

            values = {b: [f[b, rows(j), :] for j in range(SEG)] for b in blocks}
            wrapped = {b: None for b in blocks}
            for step, gone, stay, place, scale in LEVELS:
                for b in blocks:
                    v = values[b]
                    for i, j in enumerate(stay):
                        v[j] = v[j] + get(b, FWD + place + i) * v[j - step]
                        gamma = get(b, FWD + 15 + place + i)
                        if j + step < SEG:
                            v[j] = v[j] + gamma * v[j + step]
                        elif step == 1:
                            wrapped[b] = gamma * v[0]
                        else:
                            wrapped[b] = wrapped[b] + gamma * v[j + step - SEG]
            lasts = {}
            for b in blocks:
                lasts[b] = values[b][SEG - 1] + roll(wrapped[b], -1, 0)
            above = {}
            for b in blocks:
                turned = [lasts[b]] + [roll(lasts[b], k, 0) for k in range(1, SUB)]
                here = [get(b, LAST + k) * turned[k] for k in range(SUB)]
                prev = [get(b, PREV + k) * turned[k] for k in range(SUB)]
                while len(here) > 1:
                    here = [p + q for p, q in zip(here[0::2], here[1::2])]
                    prev = [p + q for p, q in zip(prev[0::2], prev[1::2])]
                values[b][SEG - 1] = here[0]
                above[b] = prev[0]
            for step, gone, stay, place, scale in reversed(LEVELS):
                for b in blocks:
                    v = values[b]
                    for i, e in enumerate(gone):
                        up = v[e - step] if e >= step else above[b]
                        src = v[e] * get(b, SCALE + scale + i) if step > 1 else v[e]
                        v[e] = src + get(b, BACK + place + i) * up + get(b, BACK + 15 + place + i) * v[e + step]
            for b in blocks:
                for j in range(SEG):
                    x[b, rows(j), :] = values[b][j]

        def relax(groups):
            def body(t, carry):
                for group in groups:
                    for b in group:
                        sources(b)
                for group in groups:
                    solve(group)
                return carry

            return body

        lax.fori_loop(0, 3, relax(((0, 1, 2), (3, 4))), 0)
        lax.fori_loop(3, 7, relax(((1, 2, 3),)), 0)
        relax(((2,),))(7, 0)

    def start_gas():
        scatter8(send_b, recv_b, 2)
        for b in (0, 1, 3, 4):
            arrive(reg_x, 4, 2, b)

    picard(reg_a, 0, True, start_gas)
    reg_c[2] = x[2]
    halo(reg_c, 1, 2, (-1, 1, -2, 2), True)

    wait_all(recv_b.at[most8], sems.at[1, 2])
    reg_b[1, 0:128, :] = unpack(recv_b, 0)
    reg_b[1, 128:256, :] = unpack(recv_b, 1)

    picard(reg_c, 1, False, lambda: halo(reg_b, 3, 1, (-1, 1), True))
    reg_d[1] = x[2]
    halo(reg_d, 2, 1, (-1, 1), True)

    def scatter4(src, dst, index):
        for tg in partners:
            remote(src.at[tg], dst.at[s], sems.at[0, index], sems.at[1, index], (tg, y)).start()

    def pack_planes(field, out, own_slot):
        tmp[...] = field.T
        for p in range(NX):
            out[p] = tmp[pl.ds(p, COLS, stride=NX), :]
        own_slot[s] = out[g]

    pack_planes(x[2], send_h, recv_h)
    scatter4(send_h, recv_h, 3)

    def gas_prepare(i, carry):
        b = (i + 1) % 3

        @pl.when(i > 0)
        def _():
            arrive(reg_b, 3, 1, b)
            arrive(reg_d, 2, 1, b)

        strip = me + b - 1
        inside = jnp.where(jnp.logical_and(strip >= 0, strip < STRIPS), 1.0, 0.0)
        a, n, r, sat, kk = TABLE
        for j in range(SEG):
            masks = zone_masks(reg_a[b + 1, pl.ds(128 + 8 * j, 8), :])
            power, one_p, mlog = saturation(reg_d[b, rows(j), :], masks)
            se = jnp.exp2(-mlog)
            span = sel(masks, [w - v for v, w in zip(r, sat)])
            inv_s = sel(masks, [1.0 / w for w in sat])
            gas = jnp.maximum(span * (1.0 - se), 1e-37)
            root = jnp.exp2((5.0 / 3.0) * jnp.log2(gas)) * inv_s * inside
            conc = reg_b[b, rows(j), :]
            gas_g[b, rows(j), :] = root
            gas_f0[b, rows(j), :] = root * conc
            gas_r[b, rows(j), :] = reg_b[b, pl.ds(128 + 8 * j, 8), :] * (sel(masks, r) + span * se) * inv_s
            gas_r[b, pl.ds(128 + 8 * j, 8), :] = GAS_STEP * inv_s
        return carry

    lax.fori_loop(0, 3, gas_prepare, 0)

    def around(ref, b, j):
        before, after = max(b - 1, 0), min(b + 1, 2)
        v = ref[b, rows(j), :]
        left = jnp.where(last_col, ref[before, rows(j), :], v)
        right = jnp.where(first_col, ref[after, rows(j), :], v)
        above = ref[b, rows(j - 1), :] if j > 0 else jnp.where(top, 0.0, roll(ref[b, rows(SEG - 1), :], 1, 0))
        below = ref[b, rows(j + 1), :] if j < SEG - 1 else jnp.where(bottom, 0.0, roll(ref[b, rows(0), :], -1, 0))
        return (
            jnp.where(first_plane, 0.0, roll(v, 1, 1))
            + jnp.where(last_plane, 0.0, roll(v, -1, 1))
            + roll(left, NX, 1)
            + roll(right, -NX, 1)
            + above
            + below
        )

    def gas_advance(b, old, flow, store):
        flux = reg_x[b + 1, pl.ds(1, 1), :]
        for j in range(SEG):
            conc = old[b, rows(j), :]
            root = gas_g[b, rows(j), :]
            if j < SEG - 1:
                under = old[b, rows(j + 1), :]
            else:
                under = jnp.where(bottom, 1.0, roll(old[b, rows(0), :], -1, 0))
            change = (
                root * (around(flow, b, j) - conc * gas_s[b, rows(j), :])
                + flux * (under - conc)
                - gas_r[b, rows(j), :] * conc
            )
            if j == 0:
                change = change + jnp.where(top, 2.0 * root * root * (1.0 - conc), 0.0)
            store(j, conc + gas_r[b, pl.ds(128 + 8 * j, 8), :] * change, root)

    for b in range(3):

        def first_store(j, new, root, b=b):
            gas_c[b, rows(j), :] = new
            gas_f1[b, rows(j), :] = root * new

        for j in range(SEG):
            gas_s[b, rows(j), :] = around(gas_g, b, j)
        gas_advance(b, reg_b, gas_f0, first_store)

    def second_store(j, new, root):
        tmp2[rows(j), :] = new

    gas_advance(1, gas_c, gas_f1, second_store)

    pack_planes(tmp2[...], send_o, recv_o)
    scatter4(send_o, recv_o, 4)

    def planes(src):
        return jnp.concatenate([src[i] for i in range(NX)], axis=0).T

    most4 = pl.ds(0, NX - 1)
    wait_all(recv_h.at[most4], sems.at[1, 3])
    field = planes(recv_h)
    for j in range(SEG):
        head_out[0, pl.ds(j, SUB, stride=SEG), :] = field[8 * j : 8 * j + 8]

    wait_all(recv_o.at[most4], sems.at[1, 4])
    field = planes(recv_o)
    for j in range(SEG):
        tmp2[pl.ds(j, SUB, stride=SEG), :] = field[8 * j : 8 * j + 8]

    def body_brick(k, c):
        ty = (y + k) % NYD
        remote(
            tmp2.at[pl.ds(pl.multiple_of(16 * ty, 16), 16)],
            brick.at[y],
            sems.at[0, 5],
            sems.at[1, 5],
            (g, ty),
        ).start()
        return c

    lax.fori_loop(1, NYD, body_brick, 0)
    brick[y] = tmp2[pl.ds(pl.multiple_of(16 * y, 16), 16), :]
    wait_all(brick.at[pl.ds(0, NYD - 1)], sems.at[1, 5])
    for i in range(NYD):
        oxy_out[0, :, 128 * i : 128 * i + 128] = brick[i]

    halo(reg_a, 0, 2, (-1, 1, -2, 2), False)
    halo(reg_x, 4, 2, (-1, 1, -2, 2), False)
    halo(reg_c, 1, 2, (-1, 1, -2, 2), False)
    halo(reg_d, 2, 1, (-1, 1), False)
    halo(reg_b, 3, 1, (-1, 1), False)
    wait_all(recv_a.at[most8], sems.at[0, 0])
    wait_all(recv_x.at[pl.ds(0, NX - 1)], sems.at[0, 1])
    wait_all(recv_b.at[most8], sems.at[0, 2])
    wait_all(recv_h.at[most4], sems.at[0, 3])
    wait_all(recv_o.at[most4], sems.at[0, 4])
    wait_all(brick.at[pl.ds(0, NYD - 1)], sems.at[0, 5])


def local(pressure_head, material_zone, emitters, oxygen, sulfide_rate, air_flux):
    vmem = pl.BlockSpec(memory_space=pltpu.VMEM)
    f32 = jnp.float32

    def buf(*shape):
        return pltpu.VMEM(shape, f32)

    block = (DEPTH, LANES)
    done = pl.pallas_call(
        kernel,
        out_shape=(
            jax.ShapeDtypeStruct((1, DEPTH, LANES), f32),
            jax.ShapeDtypeStruct((1, DEPTH // NYD, LANES * NYD), f32),
        ),
        in_specs=[pl.BlockSpec(memory_space=pl.ANY)] * 6,
        out_specs=(vmem, vmem),
        scratch_shapes=[
            buf(*block),
            buf(*block),
            buf(8 * NX, LANES),
            buf(8 * NX, LANES),
            buf(8 * NX, LANES),
            buf(8 * NX, LANES),
            buf(2, LANES),
            buf(NX, 2, LANES),
            buf(REGION, 256, LANES),
            buf(REGION, 8, LANES),
            buf(3, 256, LANES),
            buf(REGION, *block),
            buf(3, *block),
            buf(REGION, *block),
            buf(REGION, *block),
            buf(REGION, *block),
            buf(REGION, *block),
            buf(REGION, *block),
            buf(REGION, 4 * DEPTH, LANES),
            buf(REGION, *block),
            buf(REGION, *block),
            buf(REGION, *block),
            buf(REGION, 8 * NFAC, LANES),
            buf(REGION, *block),
            buf(REGION, *block),
            buf(3, *block),
            buf(3, *block),
            buf(3, *block),
            buf(3, *block),
            buf(3, *block),
            buf(3, 256, LANES),
            buf(NX, COLS, LANES),
            buf(NX, COLS, LANES),
            buf(NX, COLS, LANES),
            buf(NX, COLS, LANES),
            buf(NYD, DEPTH // NYD, LANES),
            buf(*block),
            pltpu.VMEM(block, jnp.int32),
            buf(*block),
            buf(*block),
            pltpu.VMEM((1, LANES), jnp.int32),
            buf(1, LANES),
            pltpu.SemaphoreType.DMA((2, 6)),
            pltpu.SemaphoreType.DMA((5, REGION)),
            pltpu.SemaphoreType.DMA((5, REGION)),
            pltpu.SemaphoreType.DMA((6,)),
        ],
        compiler_params=pltpu.CompilerParams(
            collective_id=0, has_side_effects=True, vmem_limit_bytes=64 * 1024 * 1024
        ),
    )(pressure_head, material_zone, emitters, oxygen, sulfide_rate, air_flux)
    return pl.pallas_call(
        finish,
        out_shape=tuple(jax.ShapeDtypeStruct(v.shape, f32) for v in done),
        in_specs=[vmem] * 2,
        out_specs=(vmem, vmem),
    )(*done)


def finish(head, oxygen, head_out, oxygen_out):
    head_out[...] = head[...]
    oxygen_out[...] = oxygen[...]


def solution(mesh):
    return jax.shard_map(
        local,
        mesh=mesh,
        in_specs=(
            P("gx", None, "gy"),
            P("gx", None, "gy"),
            P("gx", "gy"),
            P("gx", None, "gy"),
            P("gx", None, "gy"),
            P("gx", "gy"),
        ),
        out_specs=(P("gx", None, "gy"), P("gx", "gy", None)),
        check_vma=False,
    )
```

```python
import jax
import jax.numpy as jnp
from jax import lax
from jax.experimental import pallas as pl
from jax.experimental.pallas import tpu as pltpu
from jax.sharding import PartitionSpec as P

SWEEPS = 8
TABLE = (
    (4.0, 2.5, 1.2, 0.8),
    (2.4, 1.9, 1.6, 1.4),
    (0.05, 0.08, 0.1, 0.12),
    (0.38, 0.42, 0.45, 0.4),
    (5.0, 2.0, 0.6, 0.2),
)
FLOW_STEP = 2.0
STORAGE_TERM = 0.01
COND_FLOOR = 0.001
IRRIGATION = 0.3
GAS_STEP = 0.25

NX, NYD, LANES, DEPTH, SEG, SUB = 32, 8, 128, 128, 16, 8
COLS = LANES // NX
STRIPS = NX * NYD
REGION = 5
MESH = pl.DeviceIdType.MESH

FWD = 0
BACK = 30
SCALE = 60
LAST = 67
PREV = 75
NFAC = 83


def levels():
    result = []
    kept = list(range(SEG))
    place = 0
    scale = 0
    step = 1
    while len(kept) > 1:
        gone, stay = kept[0::2], kept[1::2]
        result.append((step, gone, stay, place, scale))
        place += len(gone)
        if step > 1:
            scale += len(gone)
        kept = stay
        step *= 2
    return result


LEVELS = levels()


def rows(j):
    return pl.ds(SUB * j, SUB)


def roll(x, shift, axis):
    return pltpu.roll(x, shift % x.shape[axis], axis)


def sel(masks, values):
    return jnp.where(
        masks[0],
        jnp.float32(values[0]),
        jnp.where(
            masks[1],
            jnp.float32(values[1]),
            jnp.where(masks[2], jnp.float32(values[2]), jnp.float32(values[3])),
        ),
    )


def zone_masks(zone):
    return (zone < 0.5, zone < 1.5, zone < 2.5)


def saturation(head, masks):
    a, n, r, s, k = TABLE
    au = sel(masks, a) * jnp.maximum(-head, 1e-37)
    power = jnp.exp2(sel(masks, [v - 1.0 for v in n]) * jnp.log2(au))
    one_p = 1.0 + power * au
    log_p = jnp.log2(one_p)
    m = sel(masks, [1.0 - 1.0 / v for v in n])
    return power, one_p, m * log_p


def harmonic(u, v):
    return 2.0 * u * v / (u + v)


def kernel(
    head_ref, zone_ref, em_ref, oxy_ref, sul_ref, flux_ref,
    head_out, oxy_out,
    tmp, tmp2, send_a, recv_a, send_b, recv_b, send_x, recv_x, reg_a, reg_x, reg_b, reg_c, reg_d,
    cond, half_cap, se_old, raw, base, lat, face, row_a, row_c, fac, x, f,
    gas_g, gas_s, gas_f0, gas_f1, gas_c, gas_r,
    send_h, recv_h, send_o, recv_o, in_h, in_z, in_o, in_s, in_e, in_f,
    sems, halo_s, halo_r, in_sem,
):
    g = lax.axis_index("gx")
    y = lax.axis_index("gy")

    def strip_of(gx):
        return gx + (gx // 16) * (47 - 2 * gx)

    s = strip_of(g)
    me = y * NX + s

    def device_of(strip):
        return (strip_of(strip % NX), strip // NX)

    lane = lax.broadcasted_iota(jnp.int32, (SUB, LANES), 1)
    sub = lax.broadcasted_iota(jnp.int32, (SUB, LANES), 0)
    plane = lane % NX
    col = lane // NX
    first_plane, last_plane = plane == 0, plane == NX - 1
    first_col, last_col = col == 0, col == COLS - 1
    top, bottom = sub == 0, sub == SUB - 1

    half, ring, core = g // 16, (g // 2) % 8, g % 2
    partners = [
        ((half + dh) % 2) * 16 + ((ring + dz) % 8) * 2 + (core + dc) % 2
        for dh, dz, dc in sorted(
            ((dh, dz, dc) for dh in range(2) for dz in range(8) for dc in range(2)),
            key=lambda d: (-(2 * d[0] + min(d[1], 8 - d[1])), d),
        )
        if (dh, dz, dc) != (0, 0, 0)
    ]

    barrier = pltpu.get_barrier_semaphore()

    def greet_y(k, c):
        pl.semaphore_signal(barrier, inc=1, device_id=(g, (y + k) % NYD), device_id_type=MESH)
        return c

    def valid(k):
        return jnp.logical_and(me + k >= 0, me + k < STRIPS)

    for tg in partners:
        pl.semaphore_signal(barrier, inc=1, device_id=(tg, y), device_id_type=MESH)
    lax.fori_loop(1, NYD, greet_y, 0, unroll=True)
    for k in (-1, 1, -2, 2):
        @pl.when(jnp.logical_and(valid(k), jnp.logical_or(s + k < 0, s + k >= NX)))
        def _():
            pl.semaphore_signal(barrier, inc=1, device_id=device_of(me + k), device_id_type=MESH)

    loads = [
        pltpu.make_async_copy(src.at[0], dst, in_sem.at[i])
        for i, (src, dst) in enumerate(
            ((head_ref, in_h), (zone_ref, in_z), (oxy_ref, in_o), (sul_ref, in_s))
        )
    ]
    loads.append(pltpu.make_async_copy(em_ref, in_e, in_sem.at[4]))
    loads.append(pltpu.make_async_copy(flux_ref, in_f, in_sem.at[5]))
    for load in loads:
        load.start()

    def pack(first, second, out):
        for q in range(NX // 2):
            f = first[8 * q : 8 * q + 8]
            t = second[8 * q : 8 * q + 8]
            out[pl.ds(16 * q, 8), :] = jnp.where(sub < 4, f, roll(t, 4, 0))
            out[pl.ds(16 * q + 8, 8), :] = jnp.where(sub < 4, roll(f, 4, 0), t)

    def segmented(ref):
        return jnp.concatenate(
            [ref[pl.ds(j, SUB, stride=SEG), :].astype(jnp.float32) for j in range(SEG)], axis=0
        ).T

    loads[0].wait()
    loads[1].wait()
    pack(segmented(in_h), segmented(in_z), send_a)
    loads[4].wait()
    loads[5].wait()
    send_x[0:1, :] = in_e[...].astype(jnp.float32)
    send_x[1:2, :] = in_f[...]
    own = pl.ds(pl.multiple_of(8 * g, 8), 8)
    recv_a[own, :] = send_a[pl.ds(pl.multiple_of(8 * s, 8), 8), :]
    recv_x[g] = send_x[...]

    lower = (2 - jnp.minimum(s, 2)) * jnp.minimum(y, 1)
    upper = (2 - jnp.minimum(NX - 1 - s, 2)) * jnp.minimum(NYD - 1 - y, 1)
    pl.semaphore_wait(barrier, NX - 1 + NYD - 1 + lower + upper)

    def remote(src, dst, ssem, rsem, device):
        return pltpu.make_async_remote_copy(
            src_ref=src, dst_ref=dst, send_sem=ssem, recv_sem=rsem, device_id=device, device_id_type=MESH
        )

    def scatter8(src, dst, index):
        for tg in partners:
            remote(
                src.at[pl.ds(pl.multiple_of(8 * strip_of(tg), 8), 8)],
                dst.at[pl.ds(pl.multiple_of(8 * g, 8), 8)],
                sems.at[0, index],
                sems.at[1, index],
                (tg, y),
            ).start()

    def wait_all(part, sem):
        pltpu.make_async_copy(part, part, sem).wait()

    scatter8(send_a, recv_a, 0)

    for tg in partners:
        remote(send_x, recv_x.at[g], sems.at[0, 1], sems.at[1, 1], (tg, y)).start()

    loads[2].wait()
    loads[3].wait()
    pack(segmented(in_o), segmented(in_s), send_b)
    recv_b[own, :] = send_b[pl.ds(pl.multiple_of(8 * s, 8), 8), :]

    most8 = pl.ds(0, 8 * (NX - 1))
    wait_all(recv_a.at[most8], sems.at[1, 0])

    def unpack(src, field):
        parts = [
            src[pl.ds(64 * q + 4 * field + c, 8, stride=8), :] for c in range(COLS) for q in range(NX // 8)
        ]
        return jnp.concatenate(parts, axis=0).T

    reg_a[2, 0:128, :] = unpack(recv_a, 0)
    reg_a[2, 128:256, :] = unpack(recv_a, 1)
    def halo(reg, index, middle, ks, start):
        for k in ks:
            there = middle - k

            @pl.when(valid(k))
            def _():
                copy = remote(
                    reg.at[middle],
                    reg.at[there],
                    halo_s.at[index, middle + k],
                    halo_r.at[index, there],
                    device_of(me + k),
                )
                if start:
                    copy.start()
                else:
                    copy.wait_send()

    def arrive(reg, index, middle, b):
        strip = me + b - middle
        inside = jnp.logical_and(strip >= 0, strip < STRIPS)

        @pl.when(inside)
        def _():
            pltpu.make_async_copy(reg.at[b], reg.at[b], halo_r.at[index, b]).wait()

        @pl.when(jnp.logical_not(inside))
        def _():
            reg[b] = reg[middle]

    halo(reg_a, 0, 2, (-1, 1, -2, 2), True)
    wait_all(recv_x.at[pl.ds(0, NX - 1)], sems.at[1, 1])
    tmp[0:32, :] = recv_x[:, 0, :]
    tmp[32:64, :] = recv_x[:, 1, :]
    tmp[64:128, :] = jnp.zeros((64, LANES), jnp.float32)
    tmp2[...] = tmp[...].T
    emitted = jnp.zeros((1, LANES), jnp.float32)
    fluxes = jnp.zeros((1, LANES), jnp.float32)
    lane1 = lax.broadcasted_iota(jnp.int32, (1, LANES), 1) // NX
    for c in range(COLS):
        row = tmp2[pl.ds(4 * s + c, 1), :]
        emitted = jnp.where(lane1 == c, roll(row, 32 * c, 1), emitted)
        fluxes = jnp.where(lane1 == c, roll(row, 32 * c - 32, 1), fluxes)
    reg_x[2] = jnp.concatenate(
        [emitted, fluxes, jnp.zeros((6, LANES), jnp.float32)], axis=0
    )

    halo(reg_x, 4, 2, (-1, 1, -2, 2), True)

    def picard(reg, index, first, meanwhile):
        def retain(i, carry):
            step = (i + 1) // 2
            b = 2 + step * (1 - 2 * (i % 2))

            @pl.when(i > 0)
            def _():
                arrive(reg, index, 2, b)

            for j in range(SEG):
                h = reg[b, rows(j), :]
                masks = zone_masks(reg_a[b, pl.ds(128 + 8 * j, 8), :])
                power, one_p, mlog = saturation(h, masks)
                se = jnp.exp2(-mlog)
                a, n, r, sat, kk = TABLE
                filled = power * se
                cap = (
                    sel(masks, [(w - v) * p * q * (1.0 - 1.0 / q) / FLOW_STEP for p, q, v, w in zip(a, n, r, sat)])
                    * filled
                    / one_p
                    + STORAGE_TERM / FLOW_STEP
                )
                rest = 1.0 - filled
                cond[b, rows(j), :] = sel(masks, kk) * (jnp.exp2(-0.5 * mlog) * rest * rest + COND_FLOOR)
                half_cap[b, rows(j), :] = cap
                x[b, rows(j), :] = h
                if first:
                    se_old[b, rows(j), :] = se
                    raw[b, rows(j), :] = cap * h
                else:
                    raw[b, rows(j), :] = cap * h - sel(
                        masks, [(w - v) / FLOW_STEP for v, w in zip(r, sat)]
                    ) * (se - se_old[b, rows(j), :])
            return carry

        lax.fori_loop(0, REGION, retain, 0)
        meanwhile()

        def right_faces(b, carry):
            after = jnp.minimum(b + 1, REGION - 1)
            strip = me + b - 2
            closed = jnp.logical_or(strip == -1, strip == STRIPS - 1)
            mask = jnp.where(last_col, jnp.where(closed, 0.0, 1.0), 1.0)
            for j in range(SEG):
                k = cond[b, rows(j), :]
                near = roll(jnp.where(first_col, cond[after, rows(j), :], k), -NX, 1)
                face[b, rows(j), :] = mask * harmonic(k, near)
            return carry

        lax.fori_loop(0, REGION, right_faces, 0)

        def assemble(b, carry):
            before = jnp.maximum(b - 1, 0)
            ks = [cond[b, rows(j), :] for j in range(SEG)]
            up0 = jnp.where(top, 0.0, harmonic(ks[0], roll(ks[SEG - 1], 1, 0)))
            ups = [up0] + [harmonic(ks[j], ks[j - 1]) for j in range(1, SEG)]
            los = ups[1:] + [roll(up0, -1, 0)]
            for j in range(SEG):
                k = ks[j]
                xp = jnp.where(last_plane, 0.0, harmonic(k, roll(k, -1, 1)))
                xm = roll(xp, 1, 1)
                yp = face[b, rows(j), :]
                ym = roll(jnp.where(last_col, face[before, rows(j), :], yp), NX, 1)
                diag = half_cap[b, rows(j), :] + xp + xm + yp + ym + ups[j] + los[j]
                inv = 1.0 / diag
                rhs = raw[b, rows(j), :] + ups[j] - los[j]
                if j == SEG - 1:
                    rhs = rhs - jnp.where(bottom, k, 0.0)
                if j == 0:
                    rhs = rhs + jnp.where(top, IRRIGATION * reg_x[b, pl.ds(0, 1), :], 0.0)
                base[b, rows(j), :] = rhs * inv
                lat[b, rows(j), :] = xm * inv
                lat[b, rows(SEG + j), :] = xp * inv
                lat[b, rows(2 * SEG + j), :] = ym * inv
                lat[b, rows(3 * SEG + j), :] = yp * inv
                row_a[b, rows(j), :] = ups[j] * inv
                row_c[b, rows(j), :] = los[j] * inv
            return carry

        lax.fori_loop(0, REGION, assemble, 0)

        def factor(blocks):
            state = {}
            for b in blocks:
                state[b] = (
                    [row_a[b, rows(j), :] for j in range(SEG)],
                    [None] * SEG,
                    [row_c[b, rows(j), :] for j in range(SEG)],
                )

            def put(b, i, value):
                fac[b, rows(i), :] = value

            for step, gone, stay, place, scale in LEVELS:
                for b in blocks:
                    av, bv, cv = state[b]
                    for i, e in enumerate(gone):
                        if step > 1:
                            bv[e] = 1.0 / bv[e]
                            put(b, SCALE + scale + i, bv[e])
                            av[e] = av[e] * bv[e]
                            cv[e] = cv[e] * bv[e]
                        put(b, BACK + place + i, av[e])
                        put(b, BACK + 15 + place + i, cv[e])
                for b in blocks:
                    av, bv, cv = state[b]
                    new = {}
                    for i, j in enumerate(stay):
                        up, dn = j - step, j + step
                        wrap = dn >= SEG
                        dn = dn % SEG
                        a_dn, c_dn = av[dn], cv[dn]
                        alpha, gamma = av[j], cv[j]
                        if step > 1:
                            alpha = alpha * bv[up]
                        if wrap:
                            a_dn, c_dn = roll(a_dn, -1, 0), roll(c_dn, -1, 0)
                            gamma = roll(gamma, 1, 0)
                        if step > 1:
                            gamma = gamma * bv[dn]
                        diag = (bv[j] if step > 1 else 1.0) - av[j] * cv[up] - cv[j] * a_dn
                        put(b, FWD + place + i, alpha)
                        put(b, FWD + 15 + place + i, gamma)
                        new[j] = (av[j] * av[up], diag, cv[j] * c_dn)
                    for j in stay:
                        av[j], bv[j], cv[j] = new[j]
            last = {b: (v[0][SEG - 1], v[1][SEG - 1], v[2][SEG - 1]) for b, v in state.items()}
            multipliers = {b: [] for b in blocks}
            for step in (1, 2, 4):
                for b in blocks:
                    a, d, c = last[b]
                    inv = 1.0 / d
                    alpha = a * roll(inv, step, 0)
                    gamma = c * roll(inv, -step, 0)
                    multipliers[b].append((alpha, gamma))
                    d = d - alpha * roll(c, step, 0) - gamma * roll(a, -step, 0)
                    last[b] = (alpha * roll(a, step, 0), d, gamma * roll(c, -step, 0))
            for b in blocks:
                (a1, g1), (a2, g2), (a4, g4) = multipliers[b]
                beta = a4 + g4
                inv = 1.0 / last[b][1]
                diags = [
                    None,
                    a1 + a2 * roll(g1, 2, 0),
                    a2,
                    a2 * roll(a1, 2, 0),
                    None,
                    g2 * roll(g1, -2, 0),
                    g2,
                    g1 + g2 * roll(a1, -2, 0),
                ]
                final = []
                for k in range(SUB):
                    if k == 0:
                        value = inv
                    elif k == 4:
                        value = inv * beta
                    else:
                        value = inv * (diags[k] + beta * roll(diags[(k + 4) % 8], 4, 0))
                    put(b, LAST + k, value)
                    put(b, PREV + (k + 1) % 8, roll(value, 1, 0))

        factor((0, 1, 2))
        factor((3, 4))

        def sources(b):
            before, after = max(b - 1, 0), min(b + 1, REGION - 1)
            for j in range(SEG):
                v = x[b, rows(j), :]
                left = jnp.where(last_col, x[before, rows(j), :], v)
                right = jnp.where(first_col, x[after, rows(j), :], v)
                f[b, rows(j), :] = (
                    base[b, rows(j), :]
                    + lat[b, rows(j), :] * roll(v, 1, 1)
                    + lat[b, rows(SEG + j), :] * roll(v, -1, 1)
                    + lat[b, rows(2 * SEG + j), :] * roll(left, NX, 1)
                    + lat[b, rows(3 * SEG + j), :] * roll(right, -NX, 1)
                )

        def solve(blocks):
            def get(b, i):
                return fac[b, rows(i), :]

            values = {b: [f[b, rows(j), :] for j in range(SEG)] for b in blocks}
            wrapped = {b: None for b in blocks}
            for step, gone, stay, place, scale in LEVELS:
                for b in blocks:
                    v = values[b]
                    for i, j in enumerate(stay):
                        v[j] = v[j] + get(b, FWD + place + i) * v[j - step]
                        gamma = get(b, FWD + 15 + place + i)
                        if j + step < SEG:
                            v[j] = v[j] + gamma * v[j + step]
                        elif step == 1:
                            wrapped[b] = gamma * v[0]
                        else:
                            wrapped[b] = wrapped[b] + gamma * v[j + step - SEG]
            lasts = {}
            for b in blocks:
                lasts[b] = values[b][SEG - 1] + roll(wrapped[b], -1, 0)
            above = {}
            for b in blocks:
                turned = [lasts[b]] + [roll(lasts[b], k, 0) for k in range(1, SUB)]
                here = [get(b, LAST + k) * turned[k] for k in range(SUB)]
                prev = [get(b, PREV + k) * turned[k] for k in range(SUB)]
                while len(here) > 1:
                    here = [p + q for p, q in zip(here[0::2], here[1::2])]
                    prev = [p + q for p, q in zip(prev[0::2], prev[1::2])]
                values[b][SEG - 1] = here[0]
                above[b] = prev[0]
            for step, gone, stay, place, scale in reversed(LEVELS):
                for b in blocks:
                    v = values[b]
                    for i, e in enumerate(gone):
                        up = v[e - step] if e >= step else above[b]
                        src = v[e] * get(b, SCALE + scale + i) if step > 1 else v[e]
                        v[e] = src + get(b, BACK + place + i) * up + get(b, BACK + 15 + place + i) * v[e + step]
            for b in blocks:
                for j in range(SEG):
                    x[b, rows(j), :] = values[b][j]

        def relax(groups):
            def body(t, carry):
                for group in groups:
                    for b in group:
                        sources(b)
                for group in groups:
                    solve(group)
                return carry

            return body

        lax.fori_loop(0, 3, relax(((0, 1, 2), (3, 4))), 0)
        lax.fori_loop(3, 7, relax(((1, 2, 3),)), 0)
        relax(((2,),))(7, 0)

    def start_gas():
        scatter8(send_b, recv_b, 2)
        for b in (0, 1, 3, 4):
            arrive(reg_x, 4, 2, b)

    picard(reg_a, 0, True, start_gas)
    reg_c[2] = x[2]
    halo(reg_c, 1, 2, (-1, 1, -2, 2), True)

    wait_all(recv_b.at[most8], sems.at[1, 2])
    reg_b[1, 0:128, :] = unpack(recv_b, 0)
    reg_b[1, 128:256, :] = unpack(recv_b, 1)

    picard(reg_c, 1, False, lambda: halo(reg_b, 3, 1, (-1, 1), True))
    reg_d[1] = x[2]
    halo(reg_d, 2, 1, (-1, 1), True)

    def scatter4(src, dst, index):
        for tg in partners:
            remote(src.at[tg], dst.at[s], sems.at[0, index], sems.at[1, index], (tg, y)).start()

    def pack_planes(field, out, own_slot):
        tmp[...] = field.T
        for p in range(NX):
            out[p] = tmp[pl.ds(p, COLS, stride=NX), :]
        own_slot[s] = out[g]

    pack_planes(x[2], send_h, recv_h)
    scatter4(send_h, recv_h, 3)

    def gas_prepare(i, carry):
        b = (i + 1) % 3

        @pl.when(i > 0)
        def _():
            arrive(reg_b, 3, 1, b)
            arrive(reg_d, 2, 1, b)

        strip = me + b - 1
        inside = jnp.where(jnp.logical_and(strip >= 0, strip < STRIPS), 1.0, 0.0)
        a, n, r, sat, kk = TABLE
        for j in range(SEG):
            masks = zone_masks(reg_a[b + 1, pl.ds(128 + 8 * j, 8), :])
            power, one_p, mlog = saturation(reg_d[b, rows(j), :], masks)
            se = jnp.exp2(-mlog)
            span = sel(masks, [w - v for v, w in zip(r, sat)])
            inv_s = sel(masks, [1.0 / w for w in sat])
            gas = jnp.maximum(span * (1.0 - se), 1e-37)
            root = jnp.exp2((5.0 / 3.0) * jnp.log2(gas)) * inv_s * inside
            conc = reg_b[b, rows(j), :]
            gas_g[b, rows(j), :] = root
            gas_f0[b, rows(j), :] = root * conc
            gas_r[b, rows(j), :] = reg_b[b, pl.ds(128 + 8 * j, 8), :] * (sel(masks, r) + span * se) * inv_s
            gas_r[b, pl.ds(128 + 8 * j, 8), :] = GAS_STEP * inv_s
        return carry

    lax.fori_loop(0, 3, gas_prepare, 0)

    def around(ref, b, j):
        before, after = max(b - 1, 0), min(b + 1, 2)
        v = ref[b, rows(j), :]
        left = jnp.where(last_col, ref[before, rows(j), :], v)
        right = jnp.where(first_col, ref[after, rows(j), :], v)
        above = ref[b, rows(j - 1), :] if j > 0 else jnp.where(top, 0.0, roll(ref[b, rows(SEG - 1), :], 1, 0))
        below = ref[b, rows(j + 1), :] if j < SEG - 1 else jnp.where(bottom, 0.0, roll(ref[b, rows(0), :], -1, 0))
        return (
            jnp.where(first_plane, 0.0, roll(v, 1, 1))
            + jnp.where(last_plane, 0.0, roll(v, -1, 1))
            + roll(left, NX, 1)
            + roll(right, -NX, 1)
            + above
            + below
        )

    def gas_advance(b, old, flow, store):
        flux = reg_x[b + 1, pl.ds(1, 1), :]
        for j in range(SEG):
            conc = old[b, rows(j), :]
            root = gas_g[b, rows(j), :]
            if j < SEG - 1:
                under = old[b, rows(j + 1), :]
            else:
                under = jnp.where(bottom, 1.0, roll(old[b, rows(0), :], -1, 0))
            change = (
                root * (around(flow, b, j) - conc * gas_s[b, rows(j), :])
                + flux * (under - conc)
                - gas_r[b, rows(j), :] * conc
            )
            if j == 0:
                change = change + jnp.where(top, 2.0 * root * root * (1.0 - conc), 0.0)
            store(j, conc + gas_r[b, pl.ds(128 + 8 * j, 8), :] * change, root)

    for b in range(3):

        def first_store(j, new, root, b=b):
            gas_c[b, rows(j), :] = new
            gas_f1[b, rows(j), :] = root * new

        for j in range(SEG):
            gas_s[b, rows(j), :] = around(gas_g, b, j)
        gas_advance(b, reg_b, gas_f0, first_store)

    def second_store(j, new, root):
        tmp2[rows(j), :] = new

    gas_advance(1, gas_c, gas_f1, second_store)

    pack_planes(tmp2[...], send_o, recv_o)
    scatter4(send_o, recv_o, 4)

    def planes(src):
        return jnp.concatenate([src[i] for i in range(NX)], axis=0).T

    most4 = pl.ds(0, NX - 1)
    wait_all(recv_h.at[most4], sems.at[1, 3])
    field = planes(recv_h)
    for j in range(SEG):
        in_h[pl.ds(j, SUB, stride=SEG), :] = field[8 * j : 8 * j + 8]
    result = pltpu.make_async_copy(in_h, head_out.at[0], in_sem.at[0])
    result.start()

    wait_all(recv_o.at[most4], sems.at[1, 4])
    field = planes(recv_o)
    for j in range(SEG):
        tmp2[pl.ds(j, SUB, stride=SEG), :] = field[8 * j : 8 * j + 8]

    mine = pl.ds(pl.multiple_of(LANES * y, LANES), LANES)

    def depths(b):
        return tmp2.at[pl.ds(pl.multiple_of(16 * b, 16), 16)]

    for k in (4, 5, 3, 6, 2, 7, 1):
        ty = (y + k) % NYD
        remote(depths(ty), oxy_out.at[0, :, mine], sems.at[0, 5], sems.at[1, 5], (g, ty)).start()
    kept = pltpu.make_async_copy(depths(y), oxy_out.at[0, :, mine], in_sem.at[1])
    kept.start()
    others = oxy_out.at[0, :, pl.ds(0, LANES * (NYD - 1))]
    result.wait()
    kept.wait()
    wait_all(others, sems.at[1, 5])

    halo(reg_a, 0, 2, (-1, 1, -2, 2), False)
    halo(reg_x, 4, 2, (-1, 1, -2, 2), False)
    halo(reg_c, 1, 2, (-1, 1, -2, 2), False)
    halo(reg_d, 2, 1, (-1, 1), False)
    halo(reg_b, 3, 1, (-1, 1), False)
    wait_all(recv_a.at[most8], sems.at[0, 0])
    wait_all(recv_x.at[pl.ds(0, NX - 1)], sems.at[0, 1])
    wait_all(recv_b.at[most8], sems.at[0, 2])
    wait_all(recv_h.at[most4], sems.at[0, 3])
    wait_all(recv_o.at[most4], sems.at[0, 4])
    wait_all(others, sems.at[0, 5])


def local(pressure_head, material_zone, emitters, oxygen, sulfide_rate, air_flux):
    vmem = pl.BlockSpec(memory_space=pltpu.VMEM)
    f32 = jnp.float32

    def buf(*shape):
        return pltpu.VMEM(shape, f32)

    block = (DEPTH, LANES)
    done = pl.pallas_call(
        kernel,
        out_shape=(
            jax.ShapeDtypeStruct((1, DEPTH, LANES), f32),
            jax.ShapeDtypeStruct((1, DEPTH // NYD, LANES * NYD), f32),
        ),
        in_specs=[pl.BlockSpec(memory_space=pl.ANY)] * 6,
        out_specs=(pl.BlockSpec(memory_space=pl.ANY),) * 2,
        scratch_shapes=[
            buf(*block),
            buf(*block),
            buf(8 * NX, LANES),
            buf(8 * NX, LANES),
            buf(8 * NX, LANES),
            buf(8 * NX, LANES),
            buf(2, LANES),
            buf(NX, 2, LANES),
            buf(REGION, 256, LANES),
            buf(REGION, 8, LANES),
            buf(3, 256, LANES),
            buf(REGION, *block),
            buf(3, *block),
            buf(REGION, *block),
            buf(REGION, *block),
            buf(REGION, *block),
            buf(REGION, *block),
            buf(REGION, *block),
            buf(REGION, 4 * DEPTH, LANES),
            buf(REGION, *block),
            buf(REGION, *block),
            buf(REGION, *block),
            buf(REGION, 8 * NFAC, LANES),
            buf(REGION, *block),
            buf(REGION, *block),
            buf(3, *block),
            buf(3, *block),
            buf(3, *block),
            buf(3, *block),
            buf(3, *block),
            buf(3, 256, LANES),
            buf(NX, COLS, LANES),
            buf(NX, COLS, LANES),
            buf(NX, COLS, LANES),
            buf(NX, COLS, LANES),
            buf(*block),
            pltpu.VMEM(block, jnp.int32),
            buf(*block),
            buf(*block),
            pltpu.VMEM((1, LANES), jnp.int32),
            buf(1, LANES),
            pltpu.SemaphoreType.DMA((2, 6)),
            pltpu.SemaphoreType.DMA((5, REGION)),
            pltpu.SemaphoreType.DMA((5, REGION)),
            pltpu.SemaphoreType.DMA((6,)),
        ],
        compiler_params=pltpu.CompilerParams(
            collective_id=0, has_side_effects=True, vmem_limit_bytes=64 * 1024 * 1024
        ),
    )(pressure_head, material_zone, emitters, oxygen, sulfide_rate, air_flux)
    return pl.pallas_call(
        finish,
        out_shape=tuple(jax.ShapeDtypeStruct(v.shape, f32) for v in done),
        in_specs=[vmem] * 2,
        out_specs=(vmem, vmem),
    )(*done)


def finish(head, oxygen, head_out, oxygen_out):
    head_out[...] = head[...]
    oxygen_out[...] = oxygen[...]


def solution(mesh):
    return jax.shard_map(
        local,
        mesh=mesh,
        in_specs=(
            P("gx", None, "gy"),
            P("gx", None, "gy"),
            P("gx", "gy"),
            P("gx", None, "gy"),
            P("gx", None, "gy"),
            P("gx", "gy"),
        ),
        out_specs=(P("gx", None, "gy"), P("gx", "gy", None)),
        check_vma=False,
    )
```

```python
import jax
import jax.numpy as jnp
from jax import lax
from jax.experimental import pallas as pl
from jax.experimental.pallas import tpu as pltpu
from jax.sharding import PartitionSpec as P

SWEEPS = 8
TABLE = (
    (4.0, 2.5, 1.2, 0.8),
    (2.4, 1.9, 1.6, 1.4),
    (0.05, 0.08, 0.1, 0.12),
    (0.38, 0.42, 0.45, 0.4),
    (5.0, 2.0, 0.6, 0.2),
)
FLOW_STEP = 2.0
STORAGE_TERM = 0.01
COND_FLOOR = 0.001
IRRIGATION = 0.3
GAS_STEP = 0.25

NX, NYD, LANES, DEPTH, SEG, SUB = 32, 8, 128, 128, 16, 8
COLS = LANES // NX
STRIPS = NX * NYD
REGION = 5
MESH = pl.DeviceIdType.MESH

FWD = 0
BACK = 30
SCALE = 60
LAST = 67
PREV = 75
NFAC = 83


def levels():
    result = []
    kept = list(range(SEG))
    place = 0
    scale = 0
    step = 1
    while len(kept) > 1:
        gone, stay = kept[0::2], kept[1::2]
        result.append((step, gone, stay, place, scale))
        place += len(gone)
        if step > 1:
            scale += len(gone)
        kept = stay
        step *= 2
    return result


LEVELS = levels()


def rows(j):
    return pl.ds(SUB * j, SUB)


def roll(x, shift, axis):
    return pltpu.roll(x, shift % x.shape[axis], axis)


def sel(masks, values):
    return jnp.where(
        masks[0],
        jnp.float32(values[0]),
        jnp.where(
            masks[1],
            jnp.float32(values[1]),
            jnp.where(masks[2], jnp.float32(values[2]), jnp.float32(values[3])),
        ),
    )


def zone_masks(zone):
    return (zone < 0.5, zone < 1.5, zone < 2.5)


def saturation(head, masks):
    a, n, r, s, k = TABLE
    au = sel(masks, a) * jnp.maximum(-head, 1e-37)
    power = jnp.exp2(sel(masks, [v - 1.0 for v in n]) * jnp.log2(au))
    one_p = 1.0 + power * au
    log_p = jnp.log2(one_p)
    m = sel(masks, [1.0 - 1.0 / v for v in n])
    return power, one_p, m * log_p


def harmonic(u, v):
    return 2.0 * u * v / (u + v)


def kernel(
    head_ref, zone_ref, em_ref, oxy_ref, sul_ref, flux_ref,
    head_out, oxy_out,
    tmp, tmp2, send_a, recv_a, send_b, recv_b, send_x, recv_x, reg_a, reg_x, reg_b, reg_c, reg_d,
    cond, half_cap, se_old, raw, base, lat, face, row_a, row_c, fac, x, f,
    gas_g, gas_s, gas_f0, gas_f1, gas_c, gas_r,
    send_h, recv_h, send_o, recv_o, in_h, in_z, in_o, in_s, in_e, in_f,
    sems, halo_s, halo_r, in_sem,
):
    g = lax.axis_index("gx")
    y = lax.axis_index("gy")

    def strip_of(gx):
        return gx + (gx // 16) * (47 - 2 * gx)

    s = strip_of(g)
    me = y * NX + s

    def device_of(strip):
        return (strip_of(strip % NX), strip // NX)

    lane = lax.broadcasted_iota(jnp.int32, (SUB, LANES), 1)
    sub = lax.broadcasted_iota(jnp.int32, (SUB, LANES), 0)
    plane = lane % NX
    col = lane // NX
    first_plane, last_plane = plane == 0, plane == NX - 1
    first_col, last_col = col == 0, col == COLS - 1
    top, bottom = sub == 0, sub == SUB - 1

    half, ring, core = g // 16, (g // 2) % 8, g % 2
    partners = [
        ((half + dh) % 2) * 16 + ((ring + dz) % 8) * 2 + (core + dc) % 2
        for dh, dz, dc in sorted(
            ((dh, dz, dc) for dh in range(2) for dz in range(8) for dc in range(2)),
            key=lambda d: (-(2 * d[0] + min(d[1], 8 - d[1])), d),
        )
        if (dh, dz, dc) != (0, 0, 0)
    ]

    barrier = pltpu.get_barrier_semaphore()

    def greet_y(k, c):
        pl.semaphore_signal(barrier, inc=1, device_id=(g, (y + k) % NYD), device_id_type=MESH)
        return c

    def valid(k):
        return jnp.logical_and(me + k >= 0, me + k < STRIPS)

    for tg in partners:
        pl.semaphore_signal(barrier, inc=1, device_id=(tg, y), device_id_type=MESH)
    lax.fori_loop(1, NYD, greet_y, 0, unroll=True)
    for k in (-1, 1, -2, 2):
        @pl.when(jnp.logical_and(valid(k), jnp.logical_or(s + k < 0, s + k >= NX)))
        def _():
            pl.semaphore_signal(barrier, inc=1, device_id=device_of(me + k), device_id_type=MESH)

    loads = [
        pltpu.make_async_copy(src.at[0], dst, in_sem.at[i])
        for i, (src, dst) in enumerate(
            ((head_ref, in_h), (zone_ref, in_z), (oxy_ref, in_o), (sul_ref, in_s))
        )
    ]
    loads.append(pltpu.make_async_copy(em_ref, in_e, in_sem.at[4]))
    loads.append(pltpu.make_async_copy(flux_ref, in_f, in_sem.at[5]))
    for load in loads:
        load.start()

    def pack(first, second, out):
        for q in range(NX // 2):
            f = first[8 * q : 8 * q + 8]
            t = second[8 * q : 8 * q + 8]
            out[pl.ds(16 * q, 8), :] = jnp.where(sub < 4, f, roll(t, 4, 0))
            out[pl.ds(16 * q + 8, 8), :] = jnp.where(sub < 4, roll(f, 4, 0), t)

    def segmented(ref):
        return jnp.concatenate(
            [ref[pl.ds(j, SUB, stride=SEG), :].astype(jnp.float32) for j in range(SEG)], axis=0
        ).T

    loads[0].wait()
    loads[1].wait()
    pack(segmented(in_h), segmented(in_z), send_a)
    loads[4].wait()
    loads[5].wait()
    send_x[0:1, :] = in_e[...].astype(jnp.float32)
    send_x[1:2, :] = in_f[...]
    own = pl.ds(pl.multiple_of(8 * g, 8), 8)
    recv_a[own, :] = send_a[pl.ds(pl.multiple_of(8 * s, 8), 8), :]
    recv_x[g] = send_x[...]

    lower = (2 - jnp.minimum(s, 2)) * jnp.minimum(y, 1)
    upper = (2 - jnp.minimum(NX - 1 - s, 2)) * jnp.minimum(NYD - 1 - y, 1)
    pl.semaphore_wait(barrier, NX - 1 + NYD - 1 + lower + upper)

    def remote(src, dst, ssem, rsem, device):
        return pltpu.make_async_remote_copy(
            src_ref=src, dst_ref=dst, send_sem=ssem, recv_sem=rsem, device_id=device, device_id_type=MESH
        )

    def scatter8(src, dst, index):
        for tg in partners:
            remote(
                src.at[pl.ds(pl.multiple_of(8 * strip_of(tg), 8), 8)],
                dst.at[pl.ds(pl.multiple_of(8 * g, 8), 8)],
                sems.at[0, index],
                sems.at[1, index],
                (tg, y),
            ).start()

    def wait_all(part, sem):
        pltpu.make_async_copy(part, part, sem).wait()

    scatter8(send_a, recv_a, 0)

    for tg in partners:
        remote(send_x, recv_x.at[g], sems.at[0, 1], sems.at[1, 1], (tg, y)).start()

    loads[2].wait()
    loads[3].wait()
    pack(segmented(in_o), segmented(in_s), send_b)
    recv_b[own, :] = send_b[pl.ds(pl.multiple_of(8 * s, 8), 8), :]

    most8 = pl.ds(0, 8 * (NX - 1))
    wait_all(recv_a.at[most8], sems.at[1, 0])

    def unpack(src, field):
        parts = [
            src[pl.ds(64 * q + 4 * field + c, 8, stride=8), :] for c in range(COLS) for q in range(NX // 8)
        ]
        return jnp.concatenate(parts, axis=0).T

    reg_a[2, 0:128, :] = unpack(recv_a, 0)
    reg_a[2, 128:256, :] = unpack(recv_a, 1)
    def halo(reg, index, middle, ks, start):
        for k in ks:
            there = middle - k

            @pl.when(valid(k))
            def _():
                copy = remote(
                    reg.at[middle],
                    reg.at[there],
                    halo_s.at[index, middle + k],
                    halo_r.at[index, there],
                    device_of(me + k),
                )
                if start:
                    copy.start()
                else:
                    copy.wait_send()

    def arrive(reg, index, middle, b):
        strip = me + b - middle
        inside = jnp.logical_and(strip >= 0, strip < STRIPS)

        @pl.when(inside)
        def _():
            pltpu.make_async_copy(reg.at[b], reg.at[b], halo_r.at[index, b]).wait()

        @pl.when(jnp.logical_not(inside))
        def _():
            reg[b] = reg[middle]

    halo(reg_a, 0, 2, (-1, 1, -2, 2), True)
    wait_all(recv_x.at[pl.ds(0, NX - 1)], sems.at[1, 1])
    tmp[0:32, :] = recv_x[:, 0, :]
    tmp[32:64, :] = recv_x[:, 1, :]
    tmp[64:128, :] = jnp.zeros((64, LANES), jnp.float32)
    tmp2[...] = tmp[...].T
    emitted = jnp.zeros((1, LANES), jnp.float32)
    fluxes = jnp.zeros((1, LANES), jnp.float32)
    lane1 = lax.broadcasted_iota(jnp.int32, (1, LANES), 1) // NX
    for c in range(COLS):
        row = tmp2[pl.ds(4 * s + c, 1), :]
        emitted = jnp.where(lane1 == c, roll(row, 32 * c, 1), emitted)
        fluxes = jnp.where(lane1 == c, roll(row, 32 * c - 32, 1), fluxes)
    reg_x[2] = jnp.concatenate(
        [emitted, fluxes, jnp.zeros((6, LANES), jnp.float32)], axis=0
    )

    halo(reg_x, 4, 2, (-1, 1, -2, 2), True)

    def picard(reg, index, first, meanwhile):
        def retain(i, carry):
            step = (i + 1) // 2
            b = 2 + step * (1 - 2 * (i % 2))

            @pl.when(i > 0)
            def _():
                arrive(reg, index, 2, b)

            for j in range(SEG):
                h = reg[b, rows(j), :]
                masks = zone_masks(reg_a[b, pl.ds(128 + 8 * j, 8), :])
                power, one_p, mlog = saturation(h, masks)
                se = jnp.exp2(-mlog)
                a, n, r, sat, kk = TABLE
                filled = power * se
                cap = (
                    sel(masks, [(w - v) * p * q * (1.0 - 1.0 / q) / FLOW_STEP for p, q, v, w in zip(a, n, r, sat)])
                    * filled
                    / one_p
                    + STORAGE_TERM / FLOW_STEP
                )
                rest = 1.0 - filled
                cond[b, rows(j), :] = sel(masks, kk) * (jnp.exp2(-0.5 * mlog) * rest * rest + COND_FLOOR)
                half_cap[b, rows(j), :] = cap
                x[b, rows(j), :] = h
                if first:
                    se_old[b, rows(j), :] = se
                    raw[b, rows(j), :] = cap * h
                else:
                    raw[b, rows(j), :] = cap * h - sel(
                        masks, [(w - v) / FLOW_STEP for v, w in zip(r, sat)]
                    ) * (se - se_old[b, rows(j), :])
            return carry

        lax.fori_loop(0, REGION, retain, 0)
        meanwhile()

        def right_faces(b, carry):
            after = jnp.minimum(b + 1, REGION - 1)
            strip = me + b - 2
            closed = jnp.logical_or(strip == -1, strip == STRIPS - 1)
            mask = jnp.where(last_col, jnp.where(closed, 0.0, 1.0), 1.0)
            for j in range(SEG):
                k = cond[b, rows(j), :]
                near = roll(jnp.where(first_col, cond[after, rows(j), :], k), -NX, 1)
                face[b, rows(j), :] = mask * harmonic(k, near)
            return carry

        lax.fori_loop(0, REGION, right_faces, 0)

        def assemble(b, carry):
            before = jnp.maximum(b - 1, 0)
            ks = [cond[b, rows(j), :] for j in range(SEG)]
            up0 = jnp.where(top, 0.0, harmonic(ks[0], roll(ks[SEG - 1], 1, 0)))
            ups = [up0] + [harmonic(ks[j], ks[j - 1]) for j in range(1, SEG)]
            los = ups[1:] + [roll(up0, -1, 0)]
            for j in range(SEG):
                k = ks[j]
                xp = jnp.where(last_plane, 0.0, harmonic(k, roll(k, -1, 1)))
                xm = roll(xp, 1, 1)
                yp = face[b, rows(j), :]
                ym = roll(jnp.where(last_col, face[before, rows(j), :], yp), NX, 1)
                diag = half_cap[b, rows(j), :] + xp + xm + yp + ym + ups[j] + los[j]
                inv = 1.0 / diag
                rhs = raw[b, rows(j), :] + ups[j] - los[j]
                if j == SEG - 1:
                    rhs = rhs - jnp.where(bottom, k, 0.0)
                if j == 0:
                    rhs = rhs + jnp.where(top, IRRIGATION * reg_x[b, pl.ds(0, 1), :], 0.0)
                base[b, rows(j), :] = rhs * inv
                lat[b, rows(j), :] = xm * inv
                lat[b, rows(SEG + j), :] = xp * inv
                lat[b, rows(2 * SEG + j), :] = ym * inv
                lat[b, rows(3 * SEG + j), :] = yp * inv
                row_a[b, rows(j), :] = ups[j] * inv
                row_c[b, rows(j), :] = los[j] * inv
            return carry

        lax.fori_loop(0, REGION, assemble, 0)

        def factor(blocks):
            state = {}
            for b in blocks:
                state[b] = (
                    [row_a[b, rows(j), :] for j in range(SEG)],
                    [None] * SEG,
                    [row_c[b, rows(j), :] for j in range(SEG)],
                )

            def put(b, i, value):
                fac[b, rows(i), :] = value

            for step, gone, stay, place, scale in LEVELS:
                for b in blocks:
                    av, bv, cv = state[b]
                    for i, e in enumerate(gone):
                        if step > 1:
                            bv[e] = 1.0 / bv[e]
                            put(b, SCALE + scale + i, bv[e])
                            av[e] = av[e] * bv[e]
                            cv[e] = cv[e] * bv[e]
                        put(b, BACK + place + i, av[e])
                        put(b, BACK + 15 + place + i, cv[e])
                for b in blocks:
                    av, bv, cv = state[b]
                    new = {}
                    for i, j in enumerate(stay):
                        up, dn = j - step, j + step
                        wrap = dn >= SEG
                        dn = dn % SEG
                        a_dn, c_dn = av[dn], cv[dn]
                        alpha, gamma = av[j], cv[j]
                        if step > 1:
                            alpha = alpha * bv[up]
                        if wrap:
                            a_dn, c_dn = roll(a_dn, -1, 0), roll(c_dn, -1, 0)
                            gamma = roll(gamma, 1, 0)
                        if step > 1:
                            gamma = gamma * bv[dn]
                        diag = (bv[j] if step > 1 else 1.0) - av[j] * cv[up] - cv[j] * a_dn
                        put(b, FWD + place + i, alpha)
                        put(b, FWD + 15 + place + i, gamma)
                        new[j] = (av[j] * av[up], diag, cv[j] * c_dn)
                    for j in stay:
                        av[j], bv[j], cv[j] = new[j]
            last = {b: (v[0][SEG - 1], v[1][SEG - 1], v[2][SEG - 1]) for b, v in state.items()}
            multipliers = {b: [] for b in blocks}
            for step in (1, 2, 4):
                for b in blocks:
                    a, d, c = last[b]
                    inv = 1.0 / d
                    alpha = a * roll(inv, step, 0)
                    gamma = c * roll(inv, -step, 0)
                    multipliers[b].append((alpha, gamma))
                    d = d - alpha * roll(c, step, 0) - gamma * roll(a, -step, 0)
                    last[b] = (alpha * roll(a, step, 0), d, gamma * roll(c, -step, 0))
            for b in blocks:
                (a1, g1), (a2, g2), (a4, g4) = multipliers[b]
                beta = a4 + g4
                inv = 1.0 / last[b][1]
                diags = [
                    None,
                    a1 + a2 * roll(g1, 2, 0),
                    a2,
                    a2 * roll(a1, 2, 0),
                    None,
                    g2 * roll(g1, -2, 0),
                    g2,
                    g1 + g2 * roll(a1, -2, 0),
                ]
                final = []
                for k in range(SUB):
                    if k == 0:
                        value = inv
                    elif k == 4:
                        value = inv * beta
                    else:
                        value = inv * (diags[k] + beta * roll(diags[(k + 4) % 8], 4, 0))
                    put(b, LAST + k, value)
                    put(b, PREV + (k + 1) % 8, roll(value, 1, 0))

        factor((0, 1, 2))
        factor((3, 4))

        def sources(b):
            before, after = max(b - 1, 0), min(b + 1, REGION - 1)
            for j in range(SEG):
                v = x[b, rows(j), :]
                left = jnp.where(last_col, x[before, rows(j), :], v)
                right = jnp.where(first_col, x[after, rows(j), :], v)
                f[b, rows(j), :] = (
                    base[b, rows(j), :]
                    + lat[b, rows(j), :] * roll(v, 1, 1)
                    + lat[b, rows(SEG + j), :] * roll(v, -1, 1)
                    + lat[b, rows(2 * SEG + j), :] * roll(left, NX, 1)
                    + lat[b, rows(3 * SEG + j), :] * roll(right, -NX, 1)
                )

        def solve(blocks):
            def get(b, i):
                return fac[b, rows(i), :]

            values = {b: [f[b, rows(j), :] for j in range(SEG)] for b in blocks}
            wrapped = {b: None for b in blocks}
            for step, gone, stay, place, scale in LEVELS:
                for b in blocks:
                    v = values[b]
                    for i, j in enumerate(stay):
                        v[j] = v[j] + get(b, FWD + place + i) * v[j - step]
                        gamma = get(b, FWD + 15 + place + i)
                        if j + step < SEG:
                            v[j] = v[j] + gamma * v[j + step]
                        elif step == 1:
                            wrapped[b] = gamma * v[0]
                        else:
                            wrapped[b] = wrapped[b] + gamma * v[j + step - SEG]
            lasts = {}
            for b in blocks:
                lasts[b] = values[b][SEG - 1] + roll(wrapped[b], -1, 0)
            above = {}
            for b in blocks:
                turned = [lasts[b]] + [roll(lasts[b], k, 0) for k in range(1, SUB)]
                here = [get(b, LAST + k) * turned[k] for k in range(SUB)]
                prev = [get(b, PREV + k) * turned[k] for k in range(SUB)]
                while len(here) > 1:
                    here = [p + q for p, q in zip(here[0::2], here[1::2])]
                    prev = [p + q for p, q in zip(prev[0::2], prev[1::2])]
                values[b][SEG - 1] = here[0]
                above[b] = prev[0]
            for step, gone, stay, place, scale in reversed(LEVELS):
                for b in blocks:
                    v = values[b]
                    for i, e in enumerate(gone):
                        up = v[e - step] if e >= step else above[b]
                        src = v[e] * get(b, SCALE + scale + i) if step > 1 else v[e]
                        v[e] = src + get(b, BACK + place + i) * up + get(b, BACK + 15 + place + i) * v[e + step]
            for b in blocks:
                for j in range(SEG):
                    x[b, rows(j), :] = values[b][j]

        def relax(groups):
            def body(t, carry):
                for group in groups:
                    for b in group:
                        sources(b)
                for group in groups:
                    solve(group)
                return carry

            return body

        lax.fori_loop(0, 3, relax(((0, 1, 2), (3, 4))), 0)
        lax.fori_loop(3, 7, relax(((1, 2, 3),)), 0)
        relax(((2,),))(7, 0)

    def start_gas():
        scatter8(send_b, recv_b, 2)
        for b in (0, 1, 3, 4):
            arrive(reg_x, 4, 2, b)

    picard(reg_a, 0, True, start_gas)
    reg_c[2] = x[2]
    halo(reg_c, 1, 2, (-1, 1, -2, 2), True)

    wait_all(recv_b.at[most8], sems.at[1, 2])
    reg_b[1, 0:128, :] = unpack(recv_b, 0)
    reg_b[1, 128:256, :] = unpack(recv_b, 1)

    picard(reg_c, 1, False, lambda: halo(reg_b, 3, 1, (-1, 1), True))
    reg_d[1] = x[2]
    halo(reg_d, 2, 1, (-1, 1), True)

    def scatter4(src, dst, index):
        for tg in partners:
            remote(src.at[tg], dst.at[s], sems.at[0, index], sems.at[1, index], (tg, y)).start()

    def pack_planes(field, out, own_slot):
        tmp[...] = field.T
        for p in range(NX):
            out[p] = tmp[pl.ds(p, COLS, stride=NX), :]
        own_slot[s] = out[g]

    pack_planes(x[2], send_h, recv_h)
    scatter4(send_h, recv_h, 3)

    def gas_prepare(i, carry):
        b = (i + 1) % 3

        @pl.when(i > 0)
        def _():
            arrive(reg_b, 3, 1, b)
            arrive(reg_d, 2, 1, b)

        strip = me + b - 1
        inside = jnp.where(jnp.logical_and(strip >= 0, strip < STRIPS), 1.0, 0.0)
        a, n, r, sat, kk = TABLE
        for j in range(SEG):
            masks = zone_masks(reg_a[b + 1, pl.ds(128 + 8 * j, 8), :])
            power, one_p, mlog = saturation(reg_d[b, rows(j), :], masks)
            se = jnp.exp2(-mlog)
            span = sel(masks, [w - v for v, w in zip(r, sat)])
            inv_s = sel(masks, [1.0 / w for w in sat])
            gas = jnp.maximum(span * (1.0 - se), 1e-37)
            root = jnp.exp2((5.0 / 3.0) * jnp.log2(gas)) * inv_s * inside
            conc = reg_b[b, rows(j), :]
            gas_g[b, rows(j), :] = root
            gas_f0[b, rows(j), :] = root * conc
            gas_r[b, rows(j), :] = reg_b[b, pl.ds(128 + 8 * j, 8), :] * (sel(masks, r) + span * se) * inv_s
            gas_r[b, pl.ds(128 + 8 * j, 8), :] = GAS_STEP * inv_s
        return carry

    lax.fori_loop(0, 3, gas_prepare, 0)

    def around(ref, b, j):
        before, after = max(b - 1, 0), min(b + 1, 2)
        v = ref[b, rows(j), :]
        left = jnp.where(last_col, ref[before, rows(j), :], v)
        right = jnp.where(first_col, ref[after, rows(j), :], v)
        above = ref[b, rows(j - 1), :] if j > 0 else jnp.where(top, 0.0, roll(ref[b, rows(SEG - 1), :], 1, 0))
        below = ref[b, rows(j + 1), :] if j < SEG - 1 else jnp.where(bottom, 0.0, roll(ref[b, rows(0), :], -1, 0))
        return (
            jnp.where(first_plane, 0.0, roll(v, 1, 1))
            + jnp.where(last_plane, 0.0, roll(v, -1, 1))
            + roll(left, NX, 1)
            + roll(right, -NX, 1)
            + above
            + below
        )

    def gas_advance(b, old, flow, store):
        flux = reg_x[b + 1, pl.ds(1, 1), :]
        for j in range(SEG):
            conc = old[b, rows(j), :]
            root = gas_g[b, rows(j), :]
            if j < SEG - 1:
                under = old[b, rows(j + 1), :]
            else:
                under = jnp.where(bottom, 1.0, roll(old[b, rows(0), :], -1, 0))
            change = (
                root * (around(flow, b, j) - conc * gas_s[b, rows(j), :])
                + flux * (under - conc)
                - gas_r[b, rows(j), :] * conc
            )
            if j == 0:
                change = change + jnp.where(top, 2.0 * root * root * (1.0 - conc), 0.0)
            store(j, conc + gas_r[b, pl.ds(128 + 8 * j, 8), :] * change, root)

    for b in range(3):

        def first_store(j, new, root, b=b):
            gas_c[b, rows(j), :] = new
            gas_f1[b, rows(j), :] = root * new

        for j in range(SEG):
            gas_s[b, rows(j), :] = around(gas_g, b, j)
        gas_advance(b, reg_b, gas_f0, first_store)

    def second_store(j, new, root):
        tmp2[rows(j), :] = new

    gas_advance(1, gas_c, gas_f1, second_store)

    pack_planes(tmp2[...], send_o, recv_o)
    scatter4(send_o, recv_o, 4)

    def planes(src):
        return jnp.concatenate([src[i] for i in range(NX)], axis=0).T

    most4 = pl.ds(0, NX - 1)
    halo(reg_a, 0, 2, (-1, 1, -2, 2), False)
    halo(reg_x, 4, 2, (-1, 1, -2, 2), False)
    halo(reg_c, 1, 2, (-1, 1, -2, 2), False)
    halo(reg_d, 2, 1, (-1, 1), False)
    halo(reg_b, 3, 1, (-1, 1), False)
    wait_all(recv_a.at[most8], sems.at[0, 0])
    wait_all(recv_x.at[pl.ds(0, NX - 1)], sems.at[0, 1])
    wait_all(recv_b.at[most8], sems.at[0, 2])
    wait_all(recv_h.at[most4], sems.at[1, 3])
    field = planes(recv_h)
    for j in range(SEG):
        in_h[pl.ds(j, SUB, stride=SEG), :] = field[8 * j : 8 * j + 8]
    result = pltpu.make_async_copy(in_h, head_out.at[0], in_sem.at[0])
    result.start()

    wait_all(recv_o.at[most4], sems.at[1, 4])
    field = planes(recv_o)
    for j in range(SEG):
        tmp2[pl.ds(j, SUB, stride=SEG), :] = field[8 * j : 8 * j + 8]

    mine = pl.ds(pl.multiple_of(LANES * y, LANES), LANES)

    def depths(b):
        return tmp2.at[pl.ds(pl.multiple_of(16 * b, 16), 16)]

    for k in (4, 5, 3, 6, 2, 7, 1):
        ty = (y + k) % NYD
        remote(depths(ty), oxy_out.at[0, :, mine], sems.at[0, 5], sems.at[1, 5], (g, ty)).start()
    kept = pltpu.make_async_copy(depths(y), oxy_out.at[0, :, mine], in_sem.at[1])
    kept.start()
    others = oxy_out.at[0, :, pl.ds(0, LANES * (NYD - 1))]
    wait_all(recv_h.at[most4], sems.at[0, 3])
    wait_all(recv_o.at[most4], sems.at[0, 4])
    result.wait()
    kept.wait()
    wait_all(others, sems.at[1, 5])

    wait_all(others, sems.at[0, 5])


def local(pressure_head, material_zone, emitters, oxygen, sulfide_rate, air_flux):
    vmem = pl.BlockSpec(memory_space=pltpu.VMEM)
    f32 = jnp.float32

    def buf(*shape):
        return pltpu.VMEM(shape, f32)

    block = (DEPTH, LANES)
    done = pl.pallas_call(
        kernel,
        out_shape=(
            jax.ShapeDtypeStruct((1, DEPTH, LANES), f32),
            jax.ShapeDtypeStruct((1, DEPTH // NYD, LANES * NYD), f32),
        ),
        in_specs=[pl.BlockSpec(memory_space=pl.ANY)] * 6,
        out_specs=(pl.BlockSpec(memory_space=pl.ANY),) * 2,
        scratch_shapes=[
            buf(*block),
            buf(*block),
            buf(8 * NX, LANES),
            buf(8 * NX, LANES),
            buf(8 * NX, LANES),
            buf(8 * NX, LANES),
            buf(2, LANES),
            buf(NX, 2, LANES),
            buf(REGION, 256, LANES),
            buf(REGION, 8, LANES),
            buf(3, 256, LANES),
            buf(REGION, *block),
            buf(3, *block),
            buf(REGION, *block),
            buf(REGION, *block),
            buf(REGION, *block),
            buf(REGION, *block),
            buf(REGION, *block),
            buf(REGION, 4 * DEPTH, LANES),
            buf(REGION, *block),
            buf(REGION, *block),
            buf(REGION, *block),
            buf(REGION, 8 * NFAC, LANES),
            buf(REGION, *block),
            buf(REGION, *block),
            buf(3, *block),
            buf(3, *block),
            buf(3, *block),
            buf(3, *block),
            buf(3, *block),
            buf(3, 256, LANES),
            buf(NX, COLS, LANES),
            buf(NX, COLS, LANES),
            buf(NX, COLS, LANES),
            buf(NX, COLS, LANES),
            buf(*block),
            pltpu.VMEM(block, jnp.int32),
            buf(*block),
            buf(*block),
            pltpu.VMEM((1, LANES), jnp.int32),
            buf(1, LANES),
            pltpu.SemaphoreType.DMA((2, 6)),
            pltpu.SemaphoreType.DMA((5, REGION)),
            pltpu.SemaphoreType.DMA((5, REGION)),
            pltpu.SemaphoreType.DMA((6,)),
        ],
        compiler_params=pltpu.CompilerParams(
            collective_id=0, has_side_effects=True, vmem_limit_bytes=64 * 1024 * 1024
        ),
    )(pressure_head, material_zone, emitters, oxygen, sulfide_rate, air_flux)
    return pl.pallas_call(
        finish,
        out_shape=tuple(jax.ShapeDtypeStruct(v.shape, f32) for v in done),
        in_specs=[vmem] * 2,
        out_specs=(vmem, vmem),
    )(*done)


def finish(head, oxygen, head_out, oxygen_out):
    head_out[...] = head[...]
    oxygen_out[...] = oxygen[...]


def solution(mesh):
    return jax.shard_map(
        local,
        mesh=mesh,
        in_specs=(
            P("gx", None, "gy"),
            P("gx", None, "gy"),
            P("gx", "gy"),
            P("gx", None, "gy"),
            P("gx", None, "gy"),
            P("gx", "gy"),
        ),
        out_specs=(P("gx", None, "gy"), P("gx", "gy", None)),
        check_vma=False,
    )
```

```python
import jax
import jax.numpy as jnp
from jax import lax
from jax.experimental import pallas as pl
from jax.experimental.pallas import tpu as pltpu
from jax.sharding import PartitionSpec as P

SWEEPS = 8
TABLE = (
    (4.0, 2.5, 1.2, 0.8),
    (2.4, 1.9, 1.6, 1.4),
    (0.05, 0.08, 0.1, 0.12),
    (0.38, 0.42, 0.45, 0.4),
    (5.0, 2.0, 0.6, 0.2),
)
FLOW_STEP = 2.0
STORAGE_TERM = 0.01
COND_FLOOR = 0.001
IRRIGATION = 0.3
GAS_STEP = 0.25

NX, NYD, LANES, DEPTH, SEG, SUB = 32, 8, 128, 128, 16, 8
COLS = LANES // NX
STRIPS = NX * NYD
REGION = 5
MESH = pl.DeviceIdType.MESH

FWD = 0
BACK = 30
SCALE = 60
LAST = 67
PREV = 75
NFAC = 83


def levels():
    result = []
    kept = list(range(SEG))
    place = 0
    scale = 0
    step = 1
    while len(kept) > 1:
        gone, stay = kept[0::2], kept[1::2]
        result.append((step, gone, stay, place, scale))
        place += len(gone)
        if step > 1:
            scale += len(gone)
        kept = stay
        step *= 2
    return result


LEVELS = levels()


def rows(j):
    return pl.ds(SUB * j, SUB)


def roll(x, shift, axis):
    return pltpu.roll(x, shift % x.shape[axis], axis)


def sel(masks, values):
    return jnp.where(
        masks[0],
        jnp.float32(values[0]),
        jnp.where(
            masks[1],
            jnp.float32(values[1]),
            jnp.where(masks[2], jnp.float32(values[2]), jnp.float32(values[3])),
        ),
    )


def zone_masks(zone):
    return (zone < 0.5, zone < 1.5, zone < 2.5)


def saturation(head, masks):
    a, n, r, s, k = TABLE
    au = sel(masks, a) * jnp.maximum(-head, 1e-37)
    power = jnp.exp2(sel(masks, [v - 1.0 for v in n]) * jnp.log2(au))
    one_p = 1.0 + power * au
    log_p = jnp.log2(one_p)
    m = sel(masks, [1.0 - 1.0 / v for v in n])
    return power, one_p, m * log_p


def harmonic(u, v):
    return 2.0 * u * v / (u + v)


def kernel(
    head_ref, zone_ref, em_ref, oxy_ref, sul_ref, flux_ref,
    head_out, oxy_out,
    tmp, tmp2, send_a, recv_a, send_b, recv_b, send_x, recv_x, reg_a, reg_x, reg_b, reg_c, reg_d,
    cond, half_cap, se_old, raw, base, lat, face, row_a, row_c, fac, x, f,
    gas_g, gas_s, gas_f0, gas_f1, gas_c, gas_r,
    send_h, recv_h, send_o, recv_o, in_h, in_z, in_o, in_s, in_e, in_f,
    sems, halo_s, halo_r, in_sem,
):
    g = lax.axis_index("gx")
    y = lax.axis_index("gy")

    def strip_of(gx):
        return gx + (gx // 16) * (47 - 2 * gx)

    s = strip_of(g)
    me = y * NX + s

    def device_of(strip):
        return (strip_of(strip % NX), strip // NX)

    lane = lax.broadcasted_iota(jnp.int32, (SUB, LANES), 1)
    sub = lax.broadcasted_iota(jnp.int32, (SUB, LANES), 0)
    plane = lane % NX
    col = lane // NX
    first_plane, last_plane = plane == 0, plane == NX - 1
    first_col, last_col = col == 0, col == COLS - 1
    top, bottom = sub == 0, sub == SUB - 1

    half, ring, core = g // 16, (g // 2) % 8, g % 2
    partners = [
        ((half + dh) % 2) * 16 + ((ring + dz) % 8) * 2 + (core + dc) % 2
        for dh, dz, dc in sorted(
            ((dh, dz, dc) for dh in range(2) for dz in range(8) for dc in range(2)),
            key=lambda d: (-(2 * d[0] + min(d[1], 8 - d[1])), d),
        )
        if (dh, dz, dc) != (0, 0, 0)
    ]

    barrier = pltpu.get_barrier_semaphore()

    def greet_y(k, c):
        pl.semaphore_signal(barrier, inc=1, device_id=(g, (y + k) % NYD), device_id_type=MESH)
        return c

    def valid(k):
        return jnp.logical_and(me + k >= 0, me + k < STRIPS)

    for tg in partners:
        pl.semaphore_signal(barrier, inc=1, device_id=(tg, y), device_id_type=MESH)
    lax.fori_loop(1, NYD, greet_y, 0, unroll=True)
    for k in (-1, 1, -2, 2):
        @pl.when(jnp.logical_and(valid(k), jnp.logical_or(s + k < 0, s + k >= NX)))
        def _():
            pl.semaphore_signal(barrier, inc=1, device_id=device_of(me + k), device_id_type=MESH)

    loads = [
        pltpu.make_async_copy(src.at[0], dst, in_sem.at[i])
        for i, (src, dst) in enumerate(
            ((head_ref, in_h), (zone_ref, in_z), (oxy_ref, in_o), (sul_ref, in_s))
        )
    ]
    loads.append(pltpu.make_async_copy(em_ref, in_e, in_sem.at[4]))
    loads.append(pltpu.make_async_copy(flux_ref, in_f, in_sem.at[5]))
    for load in loads:
        load.start()

    def pack(first, second, out):
        for q in range(NX // 2):
            f = first[8 * q : 8 * q + 8]
            t = second[8 * q : 8 * q + 8]
            out[pl.ds(16 * q, 8), :] = jnp.where(sub < 4, f, roll(t, 4, 0))
            out[pl.ds(16 * q + 8, 8), :] = jnp.where(sub < 4, roll(f, 4, 0), t)

    def segmented(ref):
        return jnp.concatenate(
            [ref[pl.ds(j, SUB, stride=SEG), :].astype(jnp.float32) for j in range(SEG)], axis=0
        ).T

    loads[0].wait()
    loads[1].wait()
    pack(segmented(in_h), segmented(in_z), send_a)
    loads[4].wait()
    loads[5].wait()
    send_x[0:1, :] = in_e[...].astype(jnp.float32)
    send_x[1:2, :] = in_f[...]
    own = pl.ds(pl.multiple_of(8 * g, 8), 8)
    recv_a[own, :] = send_a[pl.ds(pl.multiple_of(8 * s, 8), 8), :]
    recv_x[g] = send_x[...]

    lower = (2 - jnp.minimum(s, 2)) * jnp.minimum(y, 1)
    upper = (2 - jnp.minimum(NX - 1 - s, 2)) * jnp.minimum(NYD - 1 - y, 1)
    pl.semaphore_wait(barrier, NX - 1 + NYD - 1 + lower + upper)

    def remote(src, dst, ssem, rsem, device):
        return pltpu.make_async_remote_copy(
            src_ref=src, dst_ref=dst, send_sem=ssem, recv_sem=rsem, device_id=device, device_id_type=MESH
        )

    def scatter8(src, dst, index):
        for tg in partners:
            remote(
                src.at[pl.ds(pl.multiple_of(8 * strip_of(tg), 8), 8)],
                dst.at[pl.ds(pl.multiple_of(8 * g, 8), 8)],
                sems.at[0, index],
                sems.at[1, index],
                (tg, y),
            ).start()

    def wait_all(part, sem):
        pltpu.make_async_copy(part, part, sem).wait()

    scatter8(send_a, recv_a, 0)

    for tg in partners:
        remote(send_x, recv_x.at[g], sems.at[0, 1], sems.at[1, 1], (tg, y)).start()

    loads[2].wait()
    loads[3].wait()
    pack(segmented(in_o), segmented(in_s), send_b)
    recv_b[own, :] = send_b[pl.ds(pl.multiple_of(8 * s, 8), 8), :]

    most8 = pl.ds(0, 8 * (NX - 1))
    wait_all(recv_a.at[most8], sems.at[1, 0])

    def unpack(src, field):
        parts = [
            src[pl.ds(64 * q + 4 * field + c, 8, stride=8), :] for c in range(COLS) for q in range(NX // 8)
        ]
        return jnp.concatenate(parts, axis=0).T

    reg_a[2, 0:128, :] = unpack(recv_a, 0)
    reg_a[2, 128:256, :] = unpack(recv_a, 1)
    def halo(reg, index, middle, ks, start):
        for k in ks:
            there = middle - k

            @pl.when(valid(k))
            def _():
                copy = remote(
                    reg.at[middle],
                    reg.at[there],
                    halo_s.at[index, middle + k],
                    halo_r.at[index, there],
                    device_of(me + k),
                )
                if start:
                    copy.start()
                else:
                    copy.wait_send()

    def arrive(reg, index, middle, b):
        strip = me + b - middle
        inside = jnp.logical_and(strip >= 0, strip < STRIPS)

        @pl.when(inside)
        def _():
            pltpu.make_async_copy(reg.at[b], reg.at[b], halo_r.at[index, b]).wait()

        @pl.when(jnp.logical_not(inside))
        def _():
            reg[b] = reg[middle]

    halo(reg_a, 0, 2, (-1, 1, -2, 2), True)
    wait_all(recv_x.at[pl.ds(0, NX - 1)], sems.at[1, 1])
    tmp[0:32, :] = recv_x[:, 0, :]
    tmp[32:64, :] = recv_x[:, 1, :]
    tmp[64:128, :] = jnp.zeros((64, LANES), jnp.float32)
    tmp2[...] = tmp[...].T
    emitted = jnp.zeros((1, LANES), jnp.float32)
    fluxes = jnp.zeros((1, LANES), jnp.float32)
    lane1 = lax.broadcasted_iota(jnp.int32, (1, LANES), 1) // NX
    for c in range(COLS):
        row = tmp2[pl.ds(4 * s + c, 1), :]
        emitted = jnp.where(lane1 == c, roll(row, 32 * c, 1), emitted)
        fluxes = jnp.where(lane1 == c, roll(row, 32 * c - 32, 1), fluxes)
    reg_x[2] = jnp.concatenate(
        [emitted, fluxes, jnp.zeros((6, LANES), jnp.float32)], axis=0
    )

    halo(reg_x, 4, 2, (-1, 1, -2, 2), True)

    def picard(reg, index, first, meanwhile):
        def retain(i, carry):
            step = (i + 1) // 2
            b = 2 + step * (1 - 2 * (i % 2))

            @pl.when(i > 0)
            def _():
                arrive(reg, index, 2, b)

            for j in range(SEG):
                h = reg[b, rows(j), :]
                masks = zone_masks(reg_a[b, pl.ds(128 + 8 * j, 8), :])
                power, one_p, mlog = saturation(h, masks)
                se = jnp.exp2(-mlog)
                a, n, r, sat, kk = TABLE
                filled = power * se
                cap = (
                    sel(masks, [(w - v) * p * q * (1.0 - 1.0 / q) / FLOW_STEP for p, q, v, w in zip(a, n, r, sat)])
                    * filled
                    / one_p
                    + STORAGE_TERM / FLOW_STEP
                )
                rest = 1.0 - filled
                cond[b, rows(j), :] = sel(masks, kk) * (jnp.exp2(-0.5 * mlog) * rest * rest + COND_FLOOR)
                half_cap[b, rows(j), :] = cap
                x[b, rows(j), :] = h
                if first:
                    se_old[b, rows(j), :] = se
                    raw[b, rows(j), :] = cap * h
                else:
                    raw[b, rows(j), :] = cap * h - sel(
                        masks, [(w - v) / FLOW_STEP for v, w in zip(r, sat)]
                    ) * (se - se_old[b, rows(j), :])
            return carry


        def right_faces(b, carry):
            after = jnp.minimum(b + 1, REGION - 1)
            strip = me + b - 2
            closed = jnp.logical_or(strip == -1, strip == STRIPS - 1)
            mask = jnp.where(last_col, jnp.where(closed, 0.0, 1.0), 1.0)
            for j in range(SEG):
                k = cond[b, rows(j), :]
                near = roll(jnp.where(first_col, cond[after, rows(j), :], k), -NX, 1)
                face[b, rows(j), :] = mask * harmonic(k, near)
            return carry


        def assemble(b, carry):
            before = jnp.maximum(b - 1, 0)
            ks = [cond[b, rows(j), :] for j in range(SEG)]
            up0 = jnp.where(top, 0.0, harmonic(ks[0], roll(ks[SEG - 1], 1, 0)))
            ups = [up0] + [harmonic(ks[j], ks[j - 1]) for j in range(1, SEG)]
            los = ups[1:] + [roll(up0, -1, 0)]
            for j in range(SEG):
                k = ks[j]
                xp = jnp.where(last_plane, 0.0, harmonic(k, roll(k, -1, 1)))
                xm = roll(xp, 1, 1)
                yp = face[b, rows(j), :]
                ym = roll(jnp.where(last_col, face[before, rows(j), :], yp), NX, 1)
                diag = half_cap[b, rows(j), :] + xp + xm + yp + ym + ups[j] + los[j]
                inv = 1.0 / diag
                rhs = raw[b, rows(j), :] + ups[j] - los[j]
                if j == SEG - 1:
                    rhs = rhs - jnp.where(bottom, k, 0.0)
                if j == 0:
                    rhs = rhs + jnp.where(top, IRRIGATION * reg_x[b, pl.ds(0, 1), :], 0.0)
                base[b, rows(j), :] = rhs * inv
                lat[b, rows(j), :] = xm * inv
                lat[b, rows(SEG + j), :] = xp * inv
                lat[b, rows(2 * SEG + j), :] = ym * inv
                lat[b, rows(3 * SEG + j), :] = yp * inv
                row_a[b, rows(j), :] = ups[j] * inv
                row_c[b, rows(j), :] = los[j] * inv
            return carry


        def factor(blocks):
            state = {}
            for b in blocks:
                state[b] = (
                    [row_a[b, rows(j), :] for j in range(SEG)],
                    [None] * SEG,
                    [row_c[b, rows(j), :] for j in range(SEG)],
                )

            def put(b, i, value):
                fac[b, rows(i), :] = value

            for step, gone, stay, place, scale in LEVELS:
                for b in blocks:
                    av, bv, cv = state[b]
                    for i, e in enumerate(gone):
                        if step > 1:
                            bv[e] = 1.0 / bv[e]
                            put(b, SCALE + scale + i, bv[e])
                            av[e] = av[e] * bv[e]
                            cv[e] = cv[e] * bv[e]
                        put(b, BACK + place + i, av[e])
                        put(b, BACK + 15 + place + i, cv[e])
                for b in blocks:
                    av, bv, cv = state[b]
                    new = {}
                    for i, j in enumerate(stay):
                        up, dn = j - step, j + step
                        wrap = dn >= SEG
                        dn = dn % SEG
                        a_dn, c_dn = av[dn], cv[dn]
                        alpha, gamma = av[j], cv[j]
                        if step > 1:
                            alpha = alpha * bv[up]
                        if wrap:
                            a_dn, c_dn = roll(a_dn, -1, 0), roll(c_dn, -1, 0)
                            gamma = roll(gamma, 1, 0)
                        if step > 1:
                            gamma = gamma * bv[dn]
                        diag = (bv[j] if step > 1 else 1.0) - av[j] * cv[up] - cv[j] * a_dn
                        put(b, FWD + place + i, alpha)
                        put(b, FWD + 15 + place + i, gamma)
                        new[j] = (av[j] * av[up], diag, cv[j] * c_dn)
                    for j in stay:
                        av[j], bv[j], cv[j] = new[j]
            last = {b: (v[0][SEG - 1], v[1][SEG - 1], v[2][SEG - 1]) for b, v in state.items()}
            multipliers = {b: [] for b in blocks}
            for step in (1, 2, 4):
                for b in blocks:
                    a, d, c = last[b]
                    inv = 1.0 / d
                    alpha = a * roll(inv, step, 0)
                    gamma = c * roll(inv, -step, 0)
                    multipliers[b].append((alpha, gamma))
                    d = d - alpha * roll(c, step, 0) - gamma * roll(a, -step, 0)
                    last[b] = (alpha * roll(a, step, 0), d, gamma * roll(c, -step, 0))
            for b in blocks:
                (a1, g1), (a2, g2), (a4, g4) = multipliers[b]
                beta = a4 + g4
                inv = 1.0 / last[b][1]
                diags = [
                    None,
                    a1 + a2 * roll(g1, 2, 0),
                    a2,
                    a2 * roll(a1, 2, 0),
                    None,
                    g2 * roll(g1, -2, 0),
                    g2,
                    g1 + g2 * roll(a1, -2, 0),
                ]
                final = []
                for k in range(SUB):
                    if k == 0:
                        value = inv
                    elif k == 4:
                        value = inv * beta
                    else:
                        value = inv * (diags[k] + beta * roll(diags[(k + 4) % 8], 4, 0))
                    put(b, LAST + k, value)
                    put(b, PREV + (k + 1) % 8, roll(value, 1, 0))

        lax.fori_loop(0, 3, retain, 0)
        lax.fori_loop(1, 3, right_faces, 0)
        assemble(2, 0)
        factor((2,))
        lax.fori_loop(3, REGION, retain, 0)
        meanwhile()
        right_faces(0, 0)
        lax.fori_loop(3, REGION, right_faces, 0)
        lax.fori_loop(0, 2, assemble, 0)
        lax.fori_loop(3, REGION, assemble, 0)
        factor((0, 1, 3, 4))

        def sources(b):
            before, after = max(b - 1, 0), min(b + 1, REGION - 1)
            for j in range(SEG):
                v = x[b, rows(j), :]
                left = jnp.where(last_col, x[before, rows(j), :], v)
                right = jnp.where(first_col, x[after, rows(j), :], v)
                f[b, rows(j), :] = (
                    base[b, rows(j), :]
                    + lat[b, rows(j), :] * roll(v, 1, 1)
                    + lat[b, rows(SEG + j), :] * roll(v, -1, 1)
                    + lat[b, rows(2 * SEG + j), :] * roll(left, NX, 1)
                    + lat[b, rows(3 * SEG + j), :] * roll(right, -NX, 1)
                )

        def solve(blocks):
            def get(b, i):
                return fac[b, rows(i), :]

            values = {b: [f[b, rows(j), :] for j in range(SEG)] for b in blocks}
            wrapped = {b: None for b in blocks}
            for step, gone, stay, place, scale in LEVELS:
                for b in blocks:
                    v = values[b]
                    for i, j in enumerate(stay):
                        v[j] = v[j] + get(b, FWD + place + i) * v[j - step]
                        gamma = get(b, FWD + 15 + place + i)
                        if j + step < SEG:
                            v[j] = v[j] + gamma * v[j + step]
                        elif step == 1:
                            wrapped[b] = gamma * v[0]
                        else:
                            wrapped[b] = wrapped[b] + gamma * v[j + step - SEG]
            lasts = {}
            for b in blocks:
                lasts[b] = values[b][SEG - 1] + roll(wrapped[b], -1, 0)
            above = {}
            for b in blocks:
                turned = [lasts[b]] + [roll(lasts[b], k, 0) for k in range(1, SUB)]
                here = [get(b, LAST + k) * turned[k] for k in range(SUB)]
                prev = [get(b, PREV + k) * turned[k] for k in range(SUB)]
                while len(here) > 1:
                    here = [p + q for p, q in zip(here[0::2], here[1::2])]
                    prev = [p + q for p, q in zip(prev[0::2], prev[1::2])]
                values[b][SEG - 1] = here[0]
                above[b] = prev[0]
            for step, gone, stay, place, scale in reversed(LEVELS):
                for b in blocks:
                    v = values[b]
                    for i, e in enumerate(gone):
                        up = v[e - step] if e >= step else above[b]
                        src = v[e] * get(b, SCALE + scale + i) if step > 1 else v[e]
                        v[e] = src + get(b, BACK + place + i) * up + get(b, BACK + 15 + place + i) * v[e + step]
            for b in blocks:
                for j in range(SEG):
                    x[b, rows(j), :] = values[b][j]

        def relax(groups):
            def body(t, carry):
                for group in groups:
                    for b in group:
                        sources(b)
                for group in groups:
                    solve(group)
                return carry

            return body

        lax.fori_loop(0, 3, relax(((0, 1, 2), (3, 4))), 0)
        lax.fori_loop(3, 7, relax(((1, 2, 3),)), 0)
        relax(((2,),))(7, 0)

    def start_gas():
        scatter8(send_b, recv_b, 2)
        for b in (0, 1, 3, 4):
            arrive(reg_x, 4, 2, b)

    picard(reg_a, 0, True, start_gas)
    reg_c[2] = x[2]
    halo(reg_c, 1, 2, (-1, 1, -2, 2), True)

    wait_all(recv_b.at[most8], sems.at[1, 2])
    reg_b[1, 0:128, :] = unpack(recv_b, 0)
    reg_b[1, 128:256, :] = unpack(recv_b, 1)

    picard(reg_c, 1, False, lambda: halo(reg_b, 3, 1, (-1, 1), True))
    reg_d[1] = x[2]
    halo(reg_d, 2, 1, (-1, 1), True)

    def scatter4(src, dst, index):
        for tg in partners:
            remote(src.at[tg], dst.at[s], sems.at[0, index], sems.at[1, index], (tg, y)).start()

    def pack_planes(field, out, own_slot):
        tmp[...] = field.T
        for p in range(NX):
            out[p] = tmp[pl.ds(p, COLS, stride=NX), :]
        own_slot[s] = out[g]

    pack_planes(x[2], send_h, recv_h)
    scatter4(send_h, recv_h, 3)

    def gas_prepare(i, carry):
        b = (i + 1) % 3

        @pl.when(i > 0)
        def _():
            arrive(reg_b, 3, 1, b)
            arrive(reg_d, 2, 1, b)

        strip = me + b - 1
        inside = jnp.where(jnp.logical_and(strip >= 0, strip < STRIPS), 1.0, 0.0)
        a, n, r, sat, kk = TABLE
        for j in range(SEG):
            masks = zone_masks(reg_a[b + 1, pl.ds(128 + 8 * j, 8), :])
            power, one_p, mlog = saturation(reg_d[b, rows(j), :], masks)
            se = jnp.exp2(-mlog)
            span = sel(masks, [w - v for v, w in zip(r, sat)])
            inv_s = sel(masks, [1.0 / w for w in sat])
            gas = jnp.maximum(span * (1.0 - se), 1e-37)
            root = jnp.exp2((5.0 / 3.0) * jnp.log2(gas)) * inv_s * inside
            conc = reg_b[b, rows(j), :]
            gas_g[b, rows(j), :] = root
            gas_f0[b, rows(j), :] = root * conc
            gas_r[b, rows(j), :] = reg_b[b, pl.ds(128 + 8 * j, 8), :] * (sel(masks, r) + span * se) * inv_s
            gas_r[b, pl.ds(128 + 8 * j, 8), :] = GAS_STEP * inv_s
        return carry

    lax.fori_loop(0, 3, gas_prepare, 0)

    def around(ref, b, j):
        before, after = max(b - 1, 0), min(b + 1, 2)
        v = ref[b, rows(j), :]
        left = jnp.where(last_col, ref[before, rows(j), :], v)
        right = jnp.where(first_col, ref[after, rows(j), :], v)
        above = ref[b, rows(j - 1), :] if j > 0 else jnp.where(top, 0.0, roll(ref[b, rows(SEG - 1), :], 1, 0))
        below = ref[b, rows(j + 1), :] if j < SEG - 1 else jnp.where(bottom, 0.0, roll(ref[b, rows(0), :], -1, 0))
        return (
            jnp.where(first_plane, 0.0, roll(v, 1, 1))
            + jnp.where(last_plane, 0.0, roll(v, -1, 1))
            + roll(left, NX, 1)
            + roll(right, -NX, 1)
            + above
            + below
        )

    def gas_advance(b, old, flow, store):
        flux = reg_x[b + 1, pl.ds(1, 1), :]
        for j in range(SEG):
            conc = old[b, rows(j), :]
            root = gas_g[b, rows(j), :]
            if j < SEG - 1:
                under = old[b, rows(j + 1), :]
            else:
                under = jnp.where(bottom, 1.0, roll(old[b, rows(0), :], -1, 0))
            change = (
                root * (around(flow, b, j) - conc * gas_s[b, rows(j), :])
                + flux * (under - conc)
                - gas_r[b, rows(j), :] * conc
            )
            if j == 0:
                change = change + jnp.where(top, 2.0 * root * root * (1.0 - conc), 0.0)
            store(j, conc + gas_r[b, pl.ds(128 + 8 * j, 8), :] * change, root)

    for b in range(3):

        def first_store(j, new, root, b=b):
            gas_c[b, rows(j), :] = new
            gas_f1[b, rows(j), :] = root * new

        for j in range(SEG):
            gas_s[b, rows(j), :] = around(gas_g, b, j)
        gas_advance(b, reg_b, gas_f0, first_store)

    def second_store(j, new, root):
        tmp2[rows(j), :] = new

    gas_advance(1, gas_c, gas_f1, second_store)

    pack_planes(tmp2[...], send_o, recv_o)
    scatter4(send_o, recv_o, 4)

    def planes(src):
        return jnp.concatenate([src[i] for i in range(NX)], axis=0).T

    most4 = pl.ds(0, NX - 1)
    halo(reg_a, 0, 2, (-1, 1, -2, 2), False)
    halo(reg_x, 4, 2, (-1, 1, -2, 2), False)
    halo(reg_c, 1, 2, (-1, 1, -2, 2), False)
    halo(reg_d, 2, 1, (-1, 1), False)
    halo(reg_b, 3, 1, (-1, 1), False)
    wait_all(recv_a.at[most8], sems.at[0, 0])
    wait_all(recv_x.at[pl.ds(0, NX - 1)], sems.at[0, 1])
    wait_all(recv_b.at[most8], sems.at[0, 2])
    wait_all(recv_h.at[most4], sems.at[1, 3])
    field = planes(recv_h)
    for j in range(SEG):
        in_h[pl.ds(j, SUB, stride=SEG), :] = field[8 * j : 8 * j + 8]
    result = pltpu.make_async_copy(in_h, head_out.at[0], in_sem.at[0])
    result.start()

    wait_all(recv_o.at[most4], sems.at[1, 4])
    field = planes(recv_o)
    for j in range(SEG):
        tmp2[pl.ds(j, SUB, stride=SEG), :] = field[8 * j : 8 * j + 8]

    mine = pl.ds(pl.multiple_of(LANES * y, LANES), LANES)

    def depths(b):
        return tmp2.at[pl.ds(pl.multiple_of(16 * b, 16), 16)]

    for k in (4, 5, 3, 6, 2, 7, 1):
        ty = (y + k) % NYD
        remote(depths(ty), oxy_out.at[0, :, mine], sems.at[0, 5], sems.at[1, 5], (g, ty)).start()
    kept = pltpu.make_async_copy(depths(y), oxy_out.at[0, :, mine], in_sem.at[1])
    kept.start()
    others = oxy_out.at[0, :, pl.ds(0, LANES * (NYD - 1))]
    wait_all(recv_h.at[most4], sems.at[0, 3])
    wait_all(recv_o.at[most4], sems.at[0, 4])
    result.wait()
    kept.wait()
    wait_all(others, sems.at[1, 5])

    wait_all(others, sems.at[0, 5])


def local(pressure_head, material_zone, emitters, oxygen, sulfide_rate, air_flux):
    vmem = pl.BlockSpec(memory_space=pltpu.VMEM)
    f32 = jnp.float32

    def buf(*shape):
        return pltpu.VMEM(shape, f32)

    block = (DEPTH, LANES)
    done = pl.pallas_call(
        kernel,
        out_shape=(
            jax.ShapeDtypeStruct((1, DEPTH, LANES), f32),
            jax.ShapeDtypeStruct((1, DEPTH // NYD, LANES * NYD), f32),
        ),
        in_specs=[pl.BlockSpec(memory_space=pl.ANY)] * 6,
        out_specs=(pl.BlockSpec(memory_space=pl.ANY),) * 2,
        scratch_shapes=[
            buf(*block),
            buf(*block),
            buf(8 * NX, LANES),
            buf(8 * NX, LANES),
            buf(8 * NX, LANES),
            buf(8 * NX, LANES),
            buf(2, LANES),
            buf(NX, 2, LANES),
            buf(REGION, 256, LANES),
            buf(REGION, 8, LANES),
            buf(3, 256, LANES),
            buf(REGION, *block),
            buf(3, *block),
            buf(REGION, *block),
            buf(REGION, *block),
            buf(REGION, *block),
            buf(REGION, *block),
            buf(REGION, *block),
            buf(REGION, 4 * DEPTH, LANES),
            buf(REGION, *block),
            buf(REGION, *block),
            buf(REGION, *block),
            buf(REGION, 8 * NFAC, LANES),
            buf(REGION, *block),
            buf(REGION, *block),
            buf(3, *block),
            buf(3, *block),
            buf(3, *block),
            buf(3, *block),
            buf(3, *block),
            buf(3, 256, LANES),
            buf(NX, COLS, LANES),
            buf(NX, COLS, LANES),
            buf(NX, COLS, LANES),
            buf(NX, COLS, LANES),
            buf(*block),
            pltpu.VMEM(block, jnp.int32),
            buf(*block),
            buf(*block),
            pltpu.VMEM((1, LANES), jnp.int32),
            buf(1, LANES),
            pltpu.SemaphoreType.DMA((2, 6)),
            pltpu.SemaphoreType.DMA((5, REGION)),
            pltpu.SemaphoreType.DMA((5, REGION)),
            pltpu.SemaphoreType.DMA((6,)),
        ],
        compiler_params=pltpu.CompilerParams(
            collective_id=0, has_side_effects=True, vmem_limit_bytes=64 * 1024 * 1024
        ),
    )(pressure_head, material_zone, emitters, oxygen, sulfide_rate, air_flux)
    return pl.pallas_call(
        finish,
        out_shape=tuple(jax.ShapeDtypeStruct(v.shape, f32) for v in done),
        in_specs=[vmem] * 2,
        out_specs=(vmem, vmem),
    )(*done)


def finish(head, oxygen, head_out, oxygen_out):
    head_out[...] = head[...]
    oxygen_out[...] = oxygen[...]


def solution(mesh):
    return jax.shard_map(
        local,
        mesh=mesh,
        in_specs=(
            P("gx", None, "gy"),
            P("gx", None, "gy"),
            P("gx", "gy"),
            P("gx", None, "gy"),
            P("gx", None, "gy"),
            P("gx", "gy"),
        ),
        out_specs=(P("gx", None, "gy"), P("gx", "gy", None)),
        check_vma=False,
    )
```
